32 devices in a mesh: ctx: 8 (over z, x), head: 4 (over y, core).
Axes of the slice: x: 2, y: 2, z: 4, core: 2. Of those that a mesh axis runs over, the one named last changes fastest.
Arguments:
- hidden_in: bfloat16 [4096, 7168], P('ctx', 'head'), may hold values from -6 to 6
- gate_weight: bfloat16 [7168, 192], P('head'), may hold values from -0.09375 to 0.09375
- encoded_queries: bfloat16 [4096, 64, 128], P('ctx', 'head'), may hold values from -12 to 12
- encoded_keys: bfloat16 [4096, 4, 128], P('ctx', 'head'), may hold values from -12 to 12
- value_tensor: bfloat16 [4096, 4, 128], P('ctx', 'head'), may hold values from -6 to 6
- comp_key_weight: float32 [64, 128], replicated, may hold values from -0.75 to 0.75
- comp_value_weight: float32 [64, 128], replicated, may hold values from -0.75 to 0.75
- selection: int32 [64, 4, 16], P('ctx', 'head'), may hold values from 0 to 63, as said below
Outputs:
- attended: bfloat16 [4096, 64, 128], P('ctx', 'head')
The draws below stay inside these ranges and needn't reach their ends.
Inputs may be any that keep to these rules, and one draw needn't show every extreme that they name: `selection`: entries of one list are distinct and the first is the query block's own block. For one index of ctx and one group, the blocks named over all its query blocks that lie in one other index's shard are at most 4, and some index reaches 4 in every draw.
All inputs are finite; a program needn't handle non-finite values.
Results may differ from the reference program's by a relative error of at most 0.011.
Values may be sent and summed in bfloat16 or wider, within the bound.
A program may use at most 64 MiB of HBM per device.

```python
import jax
import jax.numpy as jnp
from jax import lax

D = 7168
QUERY_HEADS = 64
KEY_VALUE_HEADS = 4
HEAD_SIZE = 128
BLOCK_TOKENS = 64
PICKED_BLOCKS = 16
WINDOW_TOKENS = 512
CONTEXT_TOKENS = 4096
CONTEXT_BLOCKS = 64
BLOCKS_PER_INDEX = 8


def draw_encoded_queries(key, part):
    raw_values = jax.random.normal(jax.random.fold_in(key, 1), (CONTEXT_TOKENS, QUERY_HEADS, HEAD_SIZE), jnp.float32)
    return jnp.clip(raw_values, -12.0, 12.0).astype(jnp.bfloat16)


def draw_encoded_keys(key, part):
    raw_values = jax.random.normal(jax.random.fold_in(key, 11), (CONTEXT_TOKENS, KEY_VALUE_HEADS, HEAD_SIZE), jnp.float32)
    return jnp.clip(raw_values, -12.0, 12.0).astype(jnp.bfloat16)


def draw_selection(key, part):
    shard_parts = CONTEXT_BLOCKS // BLOCKS_PER_INDEX
    capacity = min(BLOCKS_PER_INDEX // 2, PICKED_BLOCKS - 1)
    pooled_scores = jax.random.randint(jax.random.fold_in(key, 21), (shard_parts, shard_parts, KEY_VALUE_HEADS, BLOCKS_PER_INDEX), 0, 1 << 20) * BLOCKS_PER_INDEX + jnp.arange(BLOCKS_PER_INDEX, dtype=jnp.int32)
    order = jnp.argsort(pooled_scores, axis=-1)
    ranks = jnp.argsort(order, axis=-1)
    in_pool = ranks < capacity
    shard_ids = jnp.arange(shard_parts, dtype=jnp.int32)
    popular_blocks_raw = jax.random.randint(jax.random.fold_in(key, 22), (shard_parts, KEY_VALUE_HEADS), 0, 1 << 20)
    hot_owner = popular_blocks_raw % jnp.maximum(shard_ids, 1)[:, None]
    block_ids = jnp.arange(CONTEXT_BLOCKS, dtype=jnp.int32)
    query_dev = block_ids // BLOCKS_PER_INDEX
    owner_dev = block_ids // BLOCKS_PER_INDEX
    local_blk = block_ids % BLOCKS_PER_INDEX
    group_index_list = jnp.arange(KEY_VALUE_HEADS, dtype=jnp.int32)
    pooled = in_pool[query_dev[:, None, None], owner_dev[None, None, :], group_index_list[None, :, None], local_blk[None, None, :]]
    eligible = (owner_dev[None, None, :] == query_dev[:, None, None]) | pooled
    causal = block_ids[None, None, :] <= block_ids[:, None, None]
    hot_match = (owner_dev[None, None, :] == hot_owner[query_dev][:, :, None]) & (owner_dev[None, None, :] != query_dev[:, None, None])
    own_block = block_ids[None, None, :] == block_ids[:, None, None]
    tier = jnp.where(own_block, 8, jnp.where(eligible & hot_match & causal, 4, jnp.where(eligible & causal, 2, jnp.where(eligible, 1, 0))))
    random_noise = jax.random.randint(jax.random.fold_in(key, 23), (CONTEXT_BLOCKS, KEY_VALUE_HEADS, CONTEXT_BLOCKS), 0, 1 << 15)
    scores = tier * (1 << 27) + random_noise * CONTEXT_BLOCKS + block_ids[None, None, :]
    chosen_vals, chosen_blocks = lax.top_k(scores, PICKED_BLOCKS)
    return chosen_blocks.astype(jnp.int32)


def with_spikes(array, rng, source, target, shards_of, factor):
    owner, partner = [(jnp.arange(array.shape[dim]) // (array.shape[dim] // shards_of)).reshape([-1 if axis == dim else 1 for axis in range(array.ndim)]) for dim in (source, target)]
    chosen = jax.random.permutation(rng, shards_of)[partner]
    strong = (owner == chosen) | (owner == (partner + shards_of // 2) % shards_of)
    return jnp.where(strong, factor * array, array)


def levels(stream_key, shape, split, least, high):
    factor_of, own = 1.0, jax.random.fold_in(stream_key, 6)
    for axis_at, blocks in split:
        steps = jnp.exp(jax.random.uniform(jax.random.fold_in(own, axis_at), (blocks,), jnp.float32, least / len(split), high / len(split)))
        factor_of = factor_of * jnp.repeat(steps, shape[axis_at] // blocks).reshape([-1 if axis == axis_at else 1 for axis in range(len(shape))])
    return factor_of


def centred(rng, extent, scale, most, cuts=(), held_as=jnp.bfloat16):
    drawn = jax.random.normal(rng, extent, jnp.float32) * scale
    if len(cuts) > 0:
        drawn = levels(rng, extent, cuts, -0.22, 0.18) * drawn
    return jnp.clip(drawn, min=-most, max=most).astype(held_as)


def heavy_noise(stream_key, dims, scale, limit, shards, heavy, held_as=jnp.bfloat16):
    array = scale * jax.random.normal(stream_key, dims, jnp.float32)
    if shards:
        array = array * levels(stream_key, dims, shards, -0.22, 0.18)
    return jnp.clip(with_spikes(array, jax.random.fold_in(stream_key, 3), *heavy), -limit, limit).astype(held_as)


def setup_inputs(seed: int = 0) -> dict:
    keys = jax.random.split(jax.random.key(seed), 9)
    return {
        "hidden_in": centred(keys[0], (CONTEXT_TOKENS, D), 1.0, 6.0, ((0, 8), (1, 4))),
        "gate_weight": heavy_noise(keys[1], (D, 3 * QUERY_HEADS), D ** -0.5, 0.09375, ((0, 4),), (0, 1, 4, 2.0)),
        "encoded_queries": draw_encoded_queries(jax.random.fold_in(keys[8], 71), 0),
        "encoded_keys": draw_encoded_keys(jax.random.fold_in(keys[8], 71), 0),
        "value_tensor": centred(keys[4], (CONTEXT_TOKENS, KEY_VALUE_HEADS, HEAD_SIZE), 1.0, 6.0, ((0, 8), (1, 4))),
        "comp_key_weight": centred(keys[5], (BLOCK_TOKENS, HEAD_SIZE), BLOCK_TOKENS ** -0.5, 0.75, (), jnp.float32),
        "comp_value_weight": centred(keys[6], (BLOCK_TOKENS, HEAD_SIZE), BLOCK_TOKENS ** -0.5, 0.75, (), jnp.float32),
        "selection": draw_selection(jax.random.fold_in(keys[8], 71), 0),
    }


def attend(query_block_index, key_rows, value_rows, key_mask, with_null):
    scale = query_block_index.shape[-1] ** -0.5
    scores = jnp.einsum("tgjd,gkd->tgjk", query_block_index.astype(jnp.float32), key_rows.astype(jnp.float32), precision=lax.Precision.HIGHEST) * scale
    scores = jnp.where(key_mask[:, :, None, :], scores, -1e30)
    peak = jnp.max(scores, axis=-1, keepdims=True)
    if with_null:
        peak = jnp.maximum(peak, 0.0)
    weights = jnp.exp(scores - peak)
    total_w = jnp.sum(weights, axis=-1, keepdims=True)
    if with_null:
        total_w = total_w + jnp.exp(-peak)
    rounded = (weights / total_w).astype(jnp.bfloat16)
    return jnp.einsum("tgjk,gkd->tgjd", rounded.astype(jnp.float32), value_rows.astype(jnp.float32), precision=lax.Precision.HIGHEST)


def reference(hidden_in, gate_weight, encoded_queries, encoded_keys, value_tensor, comp_key_weight, comp_value_weight, selection):
    block_count_total = CONTEXT_TOKENS // BLOCK_TOKENS
    group_width = QUERY_HEADS // KEY_VALUE_HEADS
    logits = jnp.dot(hidden_in, gate_weight, preferred_element_type=jnp.float32)
    gate_values = jax.nn.sigmoid(logits).reshape(CONTEXT_TOKENS, QUERY_HEADS, 3)
    widened_key_rows = encoded_keys.astype(jnp.float32).reshape(block_count_total, BLOCK_TOKENS, KEY_VALUE_HEADS, HEAD_SIZE)
    widened_value_rows = value_tensor.astype(jnp.float32).reshape(block_count_total, BLOCK_TOKENS, KEY_VALUE_HEADS, HEAD_SIZE)
    comp_keys = jnp.sum(widened_key_rows * comp_key_weight[None, :, None, :], axis=1).transpose(1, 0, 2)
    comp_values = jnp.sum(widened_value_rows * comp_value_weight[None, :, None, :], axis=1).transpose(1, 0, 2)
    comp_ends = (jnp.arange(block_count_total, dtype=jnp.int32) + 1) * BLOCK_TOKENS - 1
    blocked_keys = encoded_keys.reshape(block_count_total, BLOCK_TOKENS, KEY_VALUE_HEADS, HEAD_SIZE).transpose(2, 0, 1, 3)
    blocked_values = value_tensor.reshape(block_count_total, BLOCK_TOKENS, KEY_VALUE_HEADS, HEAD_SIZE).transpose(2, 0, 1, 3)
    padded_key_rows = jnp.concatenate([jnp.zeros((WINDOW_TOKENS, KEY_VALUE_HEADS, HEAD_SIZE), jnp.bfloat16), encoded_keys], axis=0)
    padded_value_rows = jnp.concatenate([jnp.zeros((WINDOW_TOKENS, KEY_VALUE_HEADS, HEAD_SIZE), jnp.bfloat16), value_tensor], axis=0)
    group_index_list = jnp.arange(KEY_VALUE_HEADS, dtype=jnp.int32)[:, None]
    inner_result = jnp.arange(BLOCK_TOKENS, dtype=jnp.int32)

    def per_block(block_num):
        query_start = (block_num * BLOCK_TOKENS).astype(jnp.int32)
        query_block_index = lax.dynamic_slice_in_dim(encoded_queries, query_start, BLOCK_TOKENS, 0).reshape(BLOCK_TOKENS, KEY_VALUE_HEADS, group_width, HEAD_SIZE)
        query_pos = query_start + inner_result
        comp_mask = comp_ends[None, None, :] <= query_pos[:, None, None]
        out_comp = attend(query_block_index, comp_keys, comp_values, comp_mask, True)
        chosen_blocks = selection[block_num]
        selected_keys = blocked_keys[group_index_list, chosen_blocks].reshape(KEY_VALUE_HEADS, PICKED_BLOCKS * BLOCK_TOKENS, HEAD_SIZE)
        selected_values = blocked_values[group_index_list, chosen_blocks].reshape(KEY_VALUE_HEADS, PICKED_BLOCKS * BLOCK_TOKENS, HEAD_SIZE)
        selected_positions = (chosen_blocks[:, :, None] * BLOCK_TOKENS + inner_result[None, None, :]).reshape(KEY_VALUE_HEADS, PICKED_BLOCKS * BLOCK_TOKENS)
        sel_mask = selected_positions[None, :, :] <= query_pos[:, None, None]
        out_sel = attend(query_block_index, selected_keys, selected_values, sel_mask, False)
        win_keys = lax.dynamic_slice_in_dim(padded_key_rows, query_start, WINDOW_TOKENS + BLOCK_TOKENS, 0).transpose(1, 0, 2)
        win_vals = lax.dynamic_slice_in_dim(padded_value_rows, query_start, WINDOW_TOKENS + BLOCK_TOKENS, 0).transpose(1, 0, 2)
        win_pos = query_start - WINDOW_TOKENS + jnp.arange(WINDOW_TOKENS + BLOCK_TOKENS, dtype=jnp.int32)
        win_mask = (win_pos[None, :] <= query_pos[:, None]) & (win_pos[None, :] > query_pos[:, None] - WINDOW_TOKENS) & (win_pos[None, :] >= 0)
        out_win = attend(query_block_index, win_keys, win_vals, win_mask[:, None, :], False)
        gate_block_rows = lax.dynamic_slice_in_dim(gate_values, query_start, BLOCK_TOKENS, 0).reshape(BLOCK_TOKENS, KEY_VALUE_HEADS, group_width, 3)
        merged = gate_block_rows[..., 0:1] * out_comp + gate_block_rows[..., 1:2] * out_sel + gate_block_rows[..., 2:3] * out_win
        return merged.reshape(BLOCK_TOKENS, QUERY_HEADS, HEAD_SIZE).astype(jnp.bfloat16)

    results = lax.map(per_block, jnp.arange(CONTEXT_BLOCKS, dtype=jnp.int32))
    return results.reshape(CONTEXT_TOKENS, QUERY_HEADS, HEAD_SIZE)
```

```python
import functools

import jax
import jax.numpy as jnp
from jax import lax
from jax.experimental import pallas as pl
from jax.experimental.pallas import tpu as pltpu
from jax.sharding import PartitionSpec as P

WINDOW_TOKENS = 512
NEG = -1e30
LOG2E = 1.4426950408889634
F32 = jnp.float32
BF16 = jnp.bfloat16


def dot_t(a, b):
    return lax.dot_general(a, b, (((1,), (1,)), ((), ())), preferred_element_type=F32)


def attention_kernel(
    slot_ref, valid_ref, q_ref, kv_ref, win_ref, ck_ref, cv_ref, logit_ref, out_ref, k_sel, v_sel
):
    block = kv_ref.shape[1]
    width = q_ref.shape[2]
    heads = q_ref.shape[1]
    picked = slot_ref.shape[1]
    window = WINDOW_TOKENS
    num = pl.program_id(0)
    blocks_here = pl.num_programs(0)
    first_block = lax.axis_index("ctx") * blocks_here
    own_block = first_block + num
    factor = LOG2E * width**-0.5
    own_start = window + num * block
    own_rows = win_ref[pl.ds(own_start, block), :]
    k_sel[0:block, :] = own_rows[:, :width]
    v_sel[0:block, :width] = own_rows[:, width:]
    v_sel[0:block, width:] = jnp.ones((block, width), BF16)
    own_key = jnp.broadcast_to(own_rows[0:1, :width].astype(F32), (block, width))
    for k in range(1, picked):
        keep = valid_ref[num, k].astype(F32)
        rows = kv_ref[slot_ref[num, k]].astype(F32)
        at = slice(k * block, (k + 1) * block)
        k_sel[at, :] = (jnp.where(keep > 0, rows[:, :width], own_key)).astype(BF16)
        v_sel[at, :width] = jnp.where(keep > 0, rows[:, width:], 0.0).astype(BF16)
        v_sel[at, width:] = jnp.full((block, width), keep, F32).astype(BF16)
    k_win = win_ref[pl.ds(num * block, window + block), :width]
    v_win = win_ref[pl.ds(num * block, window + block), width:]
    v_win = jnp.concatenate([v_win, jnp.ones_like(v_win)], axis=1)
    tokens = 16
    rows_n = tokens * heads
    comp_n = ck_ref.shape[0]
    for c in range(block // tokens):
        q = q_ref[c * tokens : (c + 1) * tokens].reshape(rows_n, width)
        row = lax.broadcasted_iota(jnp.int32, (rows_n, 128), 0) // heads + c * tokens
        col = lax.broadcasted_iota(jnp.int32, (rows_n, 128), 1)
        gates = jax.nn.sigmoid(logit_ref[c * tokens : (c + 1) * tokens, :])
        gates = jnp.broadcast_to(gates[:, None, :], (tokens, heads, gates.shape[1])).reshape(
            rows_n, gates.shape[1]
        )
        head = lax.broadcasted_iota(jnp.int32, gates.shape, 0) % heads
        branch = lax.broadcasted_iota(jnp.int32, gates.shape, 1) - 3 * head
        gate = [
            jnp.sum(jnp.where(branch == b, gates, 0.0), axis=1, keepdims=True) for b in range(3)
        ]
        d = dot_t(q, k_sel[...])
        d = jnp.concatenate(
            [jnp.where((col <= row) | (col >= block), d[:, :128], NEG), d[:, 128:]], axis=1
        )
        m = jnp.max(d, axis=1, keepdims=True)
        p = jnp.exp2((d - m) * factor).astype(BF16)
        acc = jnp.dot(p, v_sel[...], preferred_element_type=F32)
        total = acc[:, :width] * (gate[1] / acc[:, width:])
        d = dot_t(q, k_win)
        low = window - first_block * block - num * block
        wcol = lax.broadcasted_iota(jnp.int32, (1, window - 128), 1) + 128
        head_part = jnp.where((col > row) & (col >= low), d[:, :128], NEG)
        mid_part = d[:, 128:window] + jnp.where(wcol >= low, 0.0, NEG)
        own_part = jnp.where(col[:, :block] <= row[:, :block], d[:, window:], NEG)
        d = jnp.concatenate([head_part, mid_part, own_part], axis=1)
        m = jnp.max(d, axis=1, keepdims=True)
        p = jnp.exp2((d - m) * factor).astype(BF16)
        acc = jnp.dot(p, v_win, preferred_element_type=F32)
        total += acc[:, :width] * (gate[2] / acc[:, width:])
        d = dot_t(jnp.concatenate([q, q], axis=1), ck_ref[...])
        crow = lax.broadcasted_iota(jnp.int32, (rows_n, comp_n), 0) // heads + c * tokens
        ccol = lax.broadcasted_iota(jnp.int32, (rows_n, comp_n), 1)
        d = jnp.where((ccol + 1) * block - 1 <= crow + own_block * block, d, NEG)
        m = jnp.maximum(jnp.max(d, axis=1, keepdims=True), 0.0)
        p = jnp.exp2((d - m) * factor)
        sums = jnp.sum(p, axis=1, keepdims=True) + jnp.exp2(-m * factor)
        acc = jnp.dot(p.astype(BF16), cv_ref[...], preferred_element_type=F32)
        total += (acc[:, :width] + acc[:, width:]) * (gate[0] / sums)
        out_ref[c * tokens : (c + 1) * tokens] = total.astype(BF16).reshape(tokens, heads, width)


def attention(slots, valid, queries, kv, win, ck, cv, logits, block):
    rows, heads, width = queries.shape
    blocks_here = rows // block
    picked = slots.shape[1]
    whole = pl.BlockSpec(memory_space=pltpu.VMEM)
    scalars = pl.BlockSpec(memory_space=pltpu.SMEM)
    return pl.pallas_call(
        attention_kernel,
        grid=(blocks_here,),
        out_shape=jax.ShapeDtypeStruct(queries.shape, BF16),
        in_specs=[
            scalars,
            scalars,
            pl.BlockSpec((block, heads, width), lambda i: (i, 0, 0)),
            whole,
            whole,
            whole,
            whole,
            pl.BlockSpec((block, logits.shape[1]), lambda i: (i, 0)),
        ],
        out_specs=pl.BlockSpec((block, heads, width), lambda i: (i, 0, 0)),
        scratch_shapes=[
            pltpu.VMEM((picked * block, width), BF16),
            pltpu.VMEM((picked * block, 2 * width), BF16),
        ],
        compiler_params=pltpu.CompilerParams(vmem_limit_bytes=48 * 1024 * 1024),
        cost_estimate=pl.CostEstimate(
            flops=7_000_000_000, bytes_accessed=8_000_000, transcendentals=14_000_000
        ),
    )(slots, valid, queries, kv, win, ck, cv, logits)


def split(value):
    high = value.astype(BF16)
    return jnp.concatenate([high, (value - high.astype(F32)).astype(BF16)], axis=1)


def body(
    hidden_in,
    gate_weight,
    encoded_queries,
    encoded_keys,
    value_tensor,
    comp_key_weight,
    comp_value_weight,
    selection,
):
    rows_here, heads_here, head_dim = encoded_queries.shape
    block_len = comp_key_weight.shape[0]
    blocks_here = rows_here // block_len
    own_index = lax.axis_index("ctx")
    count = lax.axis_size("ctx")
    partial_value = jnp.dot(hidden_in, gate_weight, preferred_element_type=F32)
    logits = lax.psum_scatter(partial_value, "head", scatter_dimension=1, tiled=True)
    key_value = jnp.concatenate([encoded_keys, value_tensor], axis=-1).reshape(
        rows_here, 2 * head_dim
    )
    previous = lax.ppermute(key_value, "ctx", [(s, s + 1) for s in range(count - 1)])
    extended = jnp.concatenate([previous, key_value], axis=0)
    all_blocks = lax.all_gather(
        key_value.reshape(blocks_here, block_len, 2 * head_dim), "ctx", axis=0, tiled=True
    )
    weights = jnp.concatenate([comp_key_weight, comp_value_weight], axis=-1)
    summaries = jnp.sum(all_blocks.astype(F32) * weights[None], axis=1)
    chosen = selection[:, 0, :]
    own_blocks = own_index * blocks_here + jnp.arange(blocks_here, dtype=jnp.int32)
    valid = (chosen <= own_blocks[:, None]).astype(jnp.int32)
    return attention(
        chosen,
        valid,
        encoded_queries,
        all_blocks,
        extended,
        split(summaries[:, :head_dim]),
        split(summaries[:, head_dim:]),
        logits,
        block_len,
    )


def solution(mesh):
    return jax.shard_map(
        body,
        mesh=mesh,
        in_specs=(
            P("ctx", "head"),
            P("head", None),
            P("ctx", "head", None),
            P("ctx", "head", None),
            P("ctx", "head", None),
            P(),
            P(),
            P("ctx", "head", None),
        ),
        out_specs=P("ctx", "head", None),
        check_vma=False,
    )
```

```python
import functools

import jax
import jax.numpy as jnp
from jax import lax
from jax.experimental import pallas as pl
from jax.experimental.pallas import tpu as pltpu
from jax.sharding import PartitionSpec as P

WINDOW_TOKENS = 512
NEG = -1e30
LOG2E = 1.4426950408889634
F32 = jnp.float32
BF16 = jnp.bfloat16


def dot_t(a, b):
    return lax.dot_general(a, b, (((1,), (1,)), ((), ())), preferred_element_type=F32)


def split(value):
    high = value.astype(BF16)
    return jnp.concatenate([high, (value - high.astype(F32)).astype(BF16)], axis=1)


SLOTS = 4
MESH = pl.DeviceIdType.MESH


def exchange_kernel(
    hidden_ref,
    weight_ref,
    key_ref,
    value_ref,
    comp_ref,
    sel_ref,
    kv_ref,
    sums_ref,
    logit_ref,
    slot_ref,
    lists,
    stage,
    partial,
    parts,
    list_send,
    list_recv,
    data_send,
    data_recv,
    sums_send,
    sums_recv,
    part_send,
    part_recv,
    win_send,
    win_recv,
):
    count = lax.axis_size("ctx")
    head_count = lax.axis_size("head")
    me = lax.axis_index("ctx")
    my_head = lax.axis_index("head")
    rows, width = key_ref.shape
    block = comp_ref.shape[0]
    blocks = rows // block
    per = SLOTS * block
    base = count * per
    columns = logit_ref.shape[1]

    barrier = pltpu.get_barrier_semaphore()

    def greet(off, carry):
        pl.semaphore_signal(
            barrier, inc=1, device_id={"ctx": lax.rem(me + off, count)}, device_id_type=MESH
        )
        return carry

    lax.fori_loop(1, count, greet, 0)
    for off in range(1, head_count):
        pl.semaphore_signal(
            barrier,
            inc=1,
            device_id={"head": lax.rem(my_head + off, head_count)},
            device_id_type=MESH,
        )
    kv_ref[pl.ds(base + rows, rows), :width] = key_ref[...]
    kv_ref[pl.ds(base + rows, rows), width:] = value_ref[...]
    summary = jnp.concatenate(
        [
            jnp.sum(
                kv_ref[base + rows + n * block : base + rows + (n + 1) * block, :].astype(F32)
                * comp_ref[...],
                axis=0,
                keepdims=True,
            )
            for n in range(blocks)
        ],
        axis=0,
    )
    sums_ref[me] = summary

    @pl.when(me == 0)
    def _():
        kv_ref[base : base + rows, :] = jnp.zeros((rows, 2 * width), BF16)

    def clear(j, carry):
        sums_ref[j] = jnp.zeros(summary.shape, F32)
        return carry

    lax.fori_loop(me + 1, count, clear, 0)
    pl.semaphore_wait(barrier, count - 1 + head_count - 1)

    def list_copy(source, target):
        return pltpu.make_async_remote_copy(
            src_ref=sel_ref,
            dst_ref=lists.at[source],
            send_sem=list_send.at[target],
            recv_sem=list_recv.at[source],
            device_id={"ctx": target},
            device_id_type=MESH,
        )

    def sums_copy(source, target):
        return pltpu.make_async_remote_copy(
            src_ref=sums_ref.at[source],
            dst_ref=sums_ref.at[source],
            send_sem=sums_send.at[target],
            recv_sem=sums_recv.at[source],
            device_id={"ctx": target},
            device_id_type=MESH,
        )

    def data_copy(source, target):
        return pltpu.make_async_remote_copy(
            src_ref=stage.at[target],
            dst_ref=kv_ref.at[pl.ds(pl.multiple_of(source * per, per), per)],
            send_sem=data_send.at[target],
            recv_sem=data_recv.at[source],
            device_id={"ctx": target},
            device_id_type=MESH,
        )

    def window_copy(target):
        return pltpu.make_async_remote_copy(
            src_ref=kv_ref.at[pl.ds(base + rows, rows)],
            dst_ref=kv_ref.at[pl.ds(base, rows)],
            send_sem=win_send,
            recv_sem=win_recv,
            device_id={"ctx": target},
            device_id_type=MESH,
        )

    def part_copy(source, target):
        return pltpu.make_async_remote_copy(
            src_ref=partial.at[target],
            dst_ref=parts.at[source],
            send_sem=part_send.at[target],
            recv_sem=part_recv.at[source],
            device_id={"head": target},
            device_id_type=MESH,
        )

    def each(first, last, step):
        def run(j, carry):
            step(j)
            return carry

        lax.fori_loop(first, last, run, 0)

    each(0, me, lambda j: list_copy(me, j).start())

    @pl.when(me < count - 1)
    def _():
        window_copy(me + 1).start()

    each(me + 1, count, lambda j: sums_copy(me, j).start())

    logits = jnp.dot(hidden_ref[...], weight_ref[...], preferred_element_type=F32).T
    for h in range(head_count):
        partial[h] = logits[h * columns : (h + 1) * columns, :]
    for off in range(1, head_count):
        part_copy(my_head, lax.rem(my_head + off, head_count)).start()

    def pack(step, carry):
        target = count - 1 - step
        list_copy(target, me).wait_recv()
        wanted = lists[target]
        rank = jnp.zeros((1, 1), F32)
        places = []
        for n in range(blocks):
            need = jnp.max(
                jnp.where(wanted == me * blocks + n, 1.0, 0.0), axis=(0, 1), keepdims=True
            )
            places.append(jnp.where(need > 0, rank, -1.0))
            rank = rank + need
        for s in range(SLOTS):
            packed = jnp.zeros((block, 2 * width), F32)
            for n in range(blocks):
                rows_n = kv_ref[base + rows + n * block : base + rows + (n + 1) * block, :]
                packed = jnp.where(places[n] == s, rows_n.astype(F32), packed)
            stage[target, s * block : (s + 1) * block, :] = packed.astype(BF16)
        data_copy(me, target).start()
        return carry

    lax.fori_loop(0, count - 2 - me, pack, 0)

    @pl.when(me < count - 1)
    def _():
        list_copy(me + 1, me).wait_recv()

    mine = sel_ref[...]
    query = lax.broadcasted_iota(jnp.int32, mine.shape, 0) + me * blocks

    def place(j, slots):
        rank = jnp.zeros((1, 1), F32)
        for n in range(blocks):
            named = mine == j * blocks + n
            need = jnp.max(jnp.where(named, 1.0, 0.0), axis=(0, 1), keepdims=True)
            packed = rank.astype(jnp.int32) + j * SLOTS
            whole = count * SLOTS + n + (j - me + 1) * blocks
            place_n = jnp.where(j < me - 1, packed, whole)
            slots = jnp.where(named & (j * blocks + n <= query), place_n, slots)
            rank = rank + need
        return slots

    slot_ref[...] = lax.fori_loop(0, me + 1, place, jnp.full(mine.shape, -1, jnp.int32))

    for off in range(1, head_count):
        part_copy(lax.rem(my_head + off, head_count), my_head).wait_recv()
    total = partial[my_head]
    for off in range(1, head_count):
        total += parts[lax.rem(my_head + off, head_count)]
    logit_ref[...] = total.T

    each(0, me, lambda j: sums_copy(j, me).wait_recv())
    each(0, me - 1, lambda j: data_copy(j, me).wait_recv())

    @pl.when(me > 0)
    def _():
        window_copy(me).wait_recv()

    each(0, me, lambda j: list_copy(me, j).wait_send())
    each(me + 1, count, lambda j: sums_copy(me, j).wait_send())
    each(me + 2, count, lambda j: data_copy(me, j).wait_send())

    @pl.when(me < count - 1)
    def _():
        window_copy(me + 1).wait_send()

    for off in range(1, head_count):
        part_copy(my_head, lax.rem(my_head + off, head_count)).wait_send()


def exchange(hidden, weight, keys, values, comp, lists, count, head_count):
    rows, width = keys.shape
    block = comp.shape[0]
    blocks = rows // block
    columns = weight.shape[1] // head_count
    per = SLOTS * block
    whole = pl.BlockSpec(memory_space=pltpu.VMEM)
    dma = pltpu.SemaphoreType.DMA
    return pl.pallas_call(
        exchange_kernel,
        out_shape=(
            jax.ShapeDtypeStruct((count * per + 2 * rows, 2 * width), BF16),
            jax.ShapeDtypeStruct((count, blocks, 2 * width), F32),
            jax.ShapeDtypeStruct((rows, columns), F32),
            jax.ShapeDtypeStruct(lists.shape, jnp.int32),
        ),
        in_specs=[whole] * 6,
        out_specs=(whole,) * 4,
        scratch_shapes=[
            pltpu.VMEM((count,) + lists.shape, jnp.int32),
            pltpu.VMEM((count, per, 2 * width), BF16),
            pltpu.VMEM((head_count, columns, rows), F32),
            pltpu.VMEM((head_count, columns, rows), F32),
            dma((count,)),
            dma((count,)),
            dma((count,)),
            dma((count,)),
            dma((count,)),
            dma((count,)),
            dma((head_count,)),
            dma((head_count,)),
            dma,
            dma,
        ],
        compiler_params=pltpu.CompilerParams(
            collective_id=0, has_side_effects=True, vmem_limit_bytes=48 * 1024 * 1024
        ),
        cost_estimate=pl.CostEstimate(
            flops=400_000_000, bytes_accessed=6_000_000, transcendentals=0
        ),
    )(hidden, weight, keys, values, comp, lists)


def attention_kernel(
    slot_ref, q_ref, kv_ref, comp_ref, logit_ref, out_ref, k_sel, v_sel, ck_ref, cv_ref
):
    block = q_ref.shape[0]
    width = q_ref.shape[2]
    heads = q_ref.shape[1]
    picked = k_sel.shape[0] // block
    window = WINDOW_TOKENS
    num = pl.program_id(0)
    blocks_here = pl.num_programs(0)
    first_block = lax.axis_index("ctx") * blocks_here
    own_block = first_block + num
    factor = LOG2E * width**-0.5
    shard = blocks_here * block
    base = kv_ref.shape[0] - 2 * shard
    own_start = pl.multiple_of(base + shard + num * block, block)
    win_start = pl.multiple_of(own_start - window, block)

    @pl.when(num == 0)
    def _():
        sums = comp_ref[...].reshape(ck_ref.shape)
        ck_ref[...] = split(sums[:, :width])
        cv_ref[...] = split(sums[:, width:])

    own_rows = kv_ref[pl.ds(own_start, block), :]
    k_sel[0:block, :] = own_rows[:, :width]
    v_sel[0:block, :width] = own_rows[:, width:]
    v_sel[0:block, width:] = jnp.ones((block, width), BF16)
    own_key = jnp.broadcast_to(own_rows[0:1, :width].astype(F32), (block, width))
    for k in range(1, picked):
        slot = slot_ref[num, k]
        keep = jnp.where(slot >= 0, 1.0, 0.0)
        start = pl.multiple_of(jnp.maximum(slot, 0) * block, block)
        rows = kv_ref[pl.ds(start, block), :].astype(F32)
        at = slice(k * block, (k + 1) * block)
        k_sel[at, :] = (jnp.where(keep > 0, rows[:, :width], own_key)).astype(BF16)
        v_sel[at, :width] = jnp.where(keep > 0, rows[:, width:], 0.0).astype(BF16)
        v_sel[at, width:] = jnp.full((block, width), keep, F32).astype(BF16)
    k_win = kv_ref[pl.ds(win_start, window + block), :width]
    v_win = kv_ref[pl.ds(win_start, window + block), width:]
    v_win = jnp.concatenate([v_win, jnp.ones_like(v_win)], axis=1)
    tokens = 32
    rows_n = tokens * heads
    comp_n = ck_ref.shape[0]
    for c in range(block // tokens):
        q = q_ref[c * tokens : (c + 1) * tokens].reshape(rows_n, width)
        row = lax.broadcasted_iota(jnp.int32, (rows_n, 128), 0) // heads + c * tokens
        col = lax.broadcasted_iota(jnp.int32, (rows_n, 128), 1)
        gates = jax.nn.sigmoid(logit_ref[c * tokens : (c + 1) * tokens, :])
        gates = jnp.broadcast_to(gates[:, None, :], (tokens, heads, gates.shape[1])).reshape(
            rows_n, gates.shape[1]
        )
        head = lax.broadcasted_iota(jnp.int32, gates.shape, 0) % heads
        branch = lax.broadcasted_iota(jnp.int32, gates.shape, 1) - 3 * head
        gate = [
            jnp.sum(jnp.where(branch == b, gates, 0.0), axis=1, keepdims=True) for b in range(3)
        ]
        d = dot_t(q, k_sel[...])
        d = jnp.concatenate(
            [jnp.where((col <= row) | (col >= block), d[:, :128], NEG), d[:, 128:]], axis=1
        )
        m = jnp.max(d, axis=1, keepdims=True)
        p = jnp.exp2((d - m) * factor).astype(BF16)
        acc = jnp.dot(p, v_sel[...], preferred_element_type=F32)
        total = acc[:, :width] * (gate[1] / acc[:, width:])
        d = dot_t(q, k_win)
        low = window - first_block * block - num * block
        wcol = lax.broadcasted_iota(jnp.int32, (1, window - 128), 1) + 128
        head_part = jnp.where((col > row) & (col >= low), d[:, :128], NEG)
        mid_part = d[:, 128:window] + jnp.where(wcol >= low, 0.0, NEG)
        own_part = jnp.where(col[:, :block] <= row[:, :block], d[:, window:], NEG)
        d = jnp.concatenate([head_part, mid_part, own_part], axis=1)
        m = jnp.max(d, axis=1, keepdims=True)
        p = jnp.exp2((d - m) * factor).astype(BF16)
        acc = jnp.dot(p, v_win, preferred_element_type=F32)
        total += acc[:, :width] * (gate[2] / acc[:, width:])
        d = dot_t(jnp.concatenate([q, q], axis=1), ck_ref[...])
        crow = lax.broadcasted_iota(jnp.int32, (rows_n, comp_n), 0) // heads + c * tokens
        ccol = lax.broadcasted_iota(jnp.int32, (rows_n, comp_n), 1)
        d = jnp.where((ccol + 1) * block - 1 <= crow + own_block * block, d, NEG)
        m = jnp.maximum(jnp.max(d, axis=1, keepdims=True), 0.0)
        p = jnp.exp2((d - m) * factor)
        sums = jnp.sum(p, axis=1, keepdims=True) + jnp.exp2(-m * factor)
        acc = jnp.dot(p.astype(BF16), cv_ref[...], preferred_element_type=F32)
        total += (acc[:, :width] + acc[:, width:]) * (gate[0] / sums)
        out_ref[c * tokens : (c + 1) * tokens] = total.astype(BF16).reshape(tokens, heads, width)


def attention(slots, queries, kv, sums, logits, block, picked):
    rows, heads, width = queries.shape
    blocks_here = rows // block
    comp_n = sums.shape[0] * sums.shape[1]
    whole = pl.BlockSpec(memory_space=pltpu.VMEM)
    scalars = pl.BlockSpec(memory_space=pltpu.SMEM)
    return pl.pallas_call(
        attention_kernel,
        grid=(blocks_here,),
        out_shape=jax.ShapeDtypeStruct(queries.shape, BF16),
        in_specs=[
            scalars,
            pl.BlockSpec((block, heads, width), lambda i: (i, 0, 0)),
            whole,
            whole,
            pl.BlockSpec((block, logits.shape[1]), lambda i: (i, 0)),
        ],
        out_specs=pl.BlockSpec((block, heads, width), lambda i: (i, 0, 0)),
        scratch_shapes=[
            pltpu.VMEM((picked * block, width), BF16),
            pltpu.VMEM((picked * block, 2 * width), BF16),
            pltpu.VMEM((comp_n, 2 * width), BF16),
            pltpu.VMEM((comp_n, 2 * width), BF16),
        ],
        compiler_params=pltpu.CompilerParams(vmem_limit_bytes=48 * 1024 * 1024),
        cost_estimate=pl.CostEstimate(
            flops=7_000_000_000, bytes_accessed=8_000_000, transcendentals=14_000_000
        ),
    )(slots, queries, kv, sums, logits)


def body(
    hidden_in,
    gate_weight,
    encoded_queries,
    encoded_keys,
    value_tensor,
    comp_key_weight,
    comp_value_weight,
    selection,
):
    rows_here, heads_here, head_dim = encoded_queries.shape
    block_len = comp_key_weight.shape[0]
    picked = selection.shape[-1]
    lists = jnp.pad(selection[:, 0, :], ((0, 0), (0, 128 - picked)), constant_values=-1)
    kv, sums, logits, slots = exchange(
        hidden_in,
        gate_weight,
        encoded_keys.reshape(rows_here, head_dim),
        value_tensor.reshape(rows_here, head_dim),
        jnp.concatenate([comp_key_weight, comp_value_weight], axis=-1),
        lists,
        lax.axis_size("ctx"),
        lax.axis_size("head"),
    )
    return attention(slots, encoded_queries, kv, sums, logits, block_len, picked)


def solution(mesh):
    return jax.shard_map(
        body,
        mesh=mesh,
        in_specs=(
            P("ctx", "head"),
            P("head", None),
            P("ctx", "head", None),
            P("ctx", "head", None),
            P("ctx", "head", None),
            P(),
            P(),
            P("ctx", "head", None),
        ),
        out_specs=P("ctx", "head", None),
        check_vma=False,
    )
```

```python
import functools

import jax
import jax.numpy as jnp
from jax import lax
from jax.experimental import pallas as pl
from jax.experimental.pallas import tpu as pltpu
from jax.sharding import PartitionSpec as P

WINDOW_TOKENS = 512
NEG = -1e30
LOG2E = 1.4426950408889634
F32 = jnp.float32
BF16 = jnp.bfloat16


def dot_t(a, b):
    return lax.dot_general(a, b, (((1,), (1,)), ((), ())), preferred_element_type=F32)


def split(value):
    high = value.astype(BF16)
    return jnp.concatenate([high, (value - high.astype(F32)).astype(BF16)], axis=1)


def token_gates(logits, heads, wanted):
    tokens, columns = logits.shape
    gates = jax.nn.sigmoid(logits)
    gates = jnp.broadcast_to(gates[:, None, :], (tokens, heads, columns))
    gates = gates.reshape(tokens * heads, columns)
    head = lax.broadcasted_iota(jnp.int32, gates.shape, 0) % heads
    branch = lax.broadcasted_iota(jnp.int32, gates.shape, 1) - 3 * head
    return [
        jnp.sum(jnp.where(branch == b, gates, 0.0), axis=1, keepdims=True) for b in wanted
    ]


def near_and_comp(q, gates, k_win, v_win, ck, cv, first_token, own_block, heads, block):
    rows_n, width = q.shape
    window = WINDOW_TOKENS
    factor = LOG2E * width**-0.5
    comp_n = ck.shape[0]
    row = lax.broadcasted_iota(jnp.int32, (rows_n, 128), 0) // heads + first_token
    col = lax.broadcasted_iota(jnp.int32, (rows_n, 128), 1)
    d = dot_t(q, k_win)
    low = window - own_block * block
    wcol = lax.broadcasted_iota(jnp.int32, (1, window - 128), 1) + 128
    head_part = jnp.where((col > row) & (col >= low), d[:, :128], NEG)
    mid_part = d[:, 128:window] + jnp.where(wcol >= low, 0.0, NEG)
    own_part = jnp.where(col[:, :block] <= row[:, :block], d[:, window:], NEG)
    d = jnp.concatenate([head_part, mid_part, own_part], axis=1)
    m = jnp.max(d, axis=1, keepdims=True)
    p = jnp.exp2((d - m) * factor).astype(BF16)
    acc = jnp.dot(p, v_win, preferred_element_type=F32)
    total = acc[:, :width] * (gates[1] / acc[:, width:])
    d = dot_t(jnp.concatenate([q, q], axis=1), ck)
    crow = lax.broadcasted_iota(jnp.int32, (rows_n, comp_n), 0) // heads + first_token
    ccol = lax.broadcasted_iota(jnp.int32, (rows_n, comp_n), 1)
    d = jnp.where((ccol + 1) * block - 1 <= crow + own_block * block, d, NEG)
    m = jnp.maximum(jnp.max(d, axis=1, keepdims=True), 0.0)
    p = jnp.exp2((d - m) * factor)
    sums = jnp.sum(p, axis=1, keepdims=True) + jnp.exp2(-m * factor)
    acc = jnp.dot(p.astype(BF16), cv, preferred_element_type=F32)
    return total + (acc[:, :width] + acc[:, width:]) * (gates[0] / sums)


SLOTS = 4
MESH = pl.DeviceIdType.MESH


def exchange_kernel(
    hidden_ref,
    weight_ref,
    key_ref,
    value_ref,
    comp_key_ref,
    comp_value_ref,
    short_ref,
    query_ref,
    kv_ref,
    near_ref,
    logit_ref,
    slot_ref,
    hidden,
    queries,
    keys,
    values,
    sel_ref,
    sums_ref,
    ck_ref,
    cv_ref,
    lists,
    stage,
    partial,
    parts,
    list_send,
    list_recv,
    data_send,
    data_recv,
    sums_send,
    sums_recv,
    part_send,
    part_recv,
    win_send,
    win_recv,
    load_sem,
):
    count = lax.axis_size("ctx")
    head_count = lax.axis_size("head")
    me = lax.axis_index("ctx")
    my_head = lax.axis_index("head")
    rows, width = key_ref.shape
    block = comp_key_ref.shape[0]
    heads = query_ref.shape[1]
    blocks = rows // block
    per = SLOTS * block
    base = count * per
    columns = logit_ref.shape[1]

    loads = [
        pltpu.make_async_copy(source, target, load_sem.at[n])
        for n, (source, target) in enumerate(
            ((key_ref, keys), (value_ref, values), (hidden_ref, hidden), (query_ref, queries))
        )
    ]
    for load in loads:
        load.start()
    barrier = pltpu.get_barrier_semaphore()

    def greet(off, carry):
        pl.semaphore_signal(
            barrier, inc=1, device_id={"ctx": lax.rem(me + off, count)}, device_id_type=MESH
        )
        return carry

    lax.fori_loop(1, count, greet, 0)
    for off in range(1, head_count):
        pl.semaphore_signal(
            barrier,
            inc=1,
            device_id={"head": lax.rem(my_head + off, head_count)},
            device_id_type=MESH,
        )
    short = short_ref[...]
    sel_ref[...] = jnp.full(sel_ref.shape, -1, jnp.int32)
    sel_ref[:, : short.shape[1]] = short
    loads[0].wait()
    loads[1].wait()
    kv_ref[pl.ds(base + rows, rows), :width] = keys[...]
    kv_ref[pl.ds(base + rows, rows), width:] = values[...]
    comp_weights = jnp.concatenate([comp_key_ref[...], comp_value_ref[...]], axis=1)
    summary = jnp.concatenate(
        [
            jnp.sum(
                kv_ref[base + rows + n * block : base + rows + (n + 1) * block, :].astype(F32)
                * comp_weights,
                axis=0,
                keepdims=True,
            )
            for n in range(blocks)
        ],
        axis=0,
    )
    sums_ref[me] = summary

    @pl.when(me == 0)
    def _():
        kv_ref[base : base + rows, :] = jnp.zeros((rows, 2 * width), BF16)

    def clear(j, carry):
        sums_ref[j] = jnp.zeros(summary.shape, F32)
        return carry

    lax.fori_loop(me + 1, count, clear, 0)
    pl.semaphore_wait(barrier, count - 1 + head_count - 1)

    def list_copy(source, target):
        return pltpu.make_async_remote_copy(
            src_ref=sel_ref,
            dst_ref=lists.at[source],
            send_sem=list_send.at[target],
            recv_sem=list_recv.at[source],
            device_id={"ctx": target},
            device_id_type=MESH,
        )

    def sums_copy(source, target):
        return pltpu.make_async_remote_copy(
            src_ref=sums_ref.at[source],
            dst_ref=sums_ref.at[source],
            send_sem=sums_send.at[target],
            recv_sem=sums_recv.at[source],
            device_id={"ctx": target},
            device_id_type=MESH,
        )

    def data_copy(source, target):
        return pltpu.make_async_remote_copy(
            src_ref=stage.at[target],
            dst_ref=kv_ref.at[pl.ds(pl.multiple_of(source * per, per), per)],
            send_sem=data_send.at[target],
            recv_sem=data_recv.at[source],
            device_id={"ctx": target},
            device_id_type=MESH,
        )

    def window_copy(target):
        return pltpu.make_async_remote_copy(
            src_ref=kv_ref.at[pl.ds(base + rows, rows)],
            dst_ref=kv_ref.at[pl.ds(base, rows)],
            send_sem=win_send,
            recv_sem=win_recv,
            device_id={"ctx": target},
            device_id_type=MESH,
        )

    def part_copy(source, target):
        return pltpu.make_async_remote_copy(
            src_ref=partial.at[target],
            dst_ref=parts.at[source],
            send_sem=part_send.at[target],
            recv_sem=part_recv.at[source],
            device_id={"head": target},
            device_id_type=MESH,
        )

    def each(first, last, step):
        def run(j, carry):
            step(j)
            return carry

        lax.fori_loop(first, last, run, 0)

    each(0, me, lambda j: list_copy(me, j).start())

    @pl.when(me < count - 1)
    def _():
        window_copy(me + 1).start()

    each(me + 1, count, lambda j: sums_copy(me, j).start())

    loads[2].wait()
    logits = dot_t(weight_ref[...], hidden[...])
    for h in range(head_count):
        partial[h] = logits[h * columns : (h + 1) * columns, :]
    for off in range(1, head_count):
        part_copy(my_head, lax.rem(my_head + off, head_count)).start()

    def pack(step, carry):
        target = count - 1 - step
        list_copy(target, me).wait_recv()
        wanted = lists[target]
        rank = jnp.zeros((1, 1), F32)
        places = []
        for n in range(blocks):
            need = jnp.max(
                jnp.where(wanted == me * blocks + n, 1.0, 0.0), axis=(0, 1), keepdims=True
            )
            places.append(jnp.where(need > 0, rank, -1.0))
            rank = rank + need
        for s in range(SLOTS):
            packed = jnp.zeros((block, 2 * width), F32)
            for n in range(blocks):
                rows_n = kv_ref[base + rows + n * block : base + rows + (n + 1) * block, :]
                packed = jnp.where(places[n] == s, rows_n.astype(F32), packed)
            stage[target, s * block : (s + 1) * block, :] = packed.astype(BF16)
        data_copy(me, target).start()
        return carry

    lax.fori_loop(0, count - 2 - me, pack, 0)

    @pl.when(me < count - 1)
    def _():
        list_copy(me + 1, me).wait_recv()

    mine = sel_ref[...]
    query = lax.broadcasted_iota(jnp.int32, mine.shape, 0) + me * blocks

    def place(j, slots):
        rank = jnp.zeros((1, 1), F32)
        for n in range(blocks):
            named = mine == j * blocks + n
            need = jnp.max(jnp.where(named, 1.0, 0.0), axis=(0, 1), keepdims=True)
            packed = rank.astype(jnp.int32) + j * SLOTS
            whole = count * SLOTS + n + (j - me + 1) * blocks
            place_n = jnp.where(j < me - 1, packed, whole)
            slots = jnp.where(named & (j * blocks + n <= query), place_n, slots)
            rank = rank + need
        return slots

    slot_ref[...] = lax.fori_loop(0, me + 1, place, jnp.full(mine.shape, -1, jnp.int32))

    for off in range(1, head_count):
        part_copy(lax.rem(my_head + off, head_count), my_head).wait_recv()
    total = partial[my_head]
    for off in range(1, head_count):
        total += parts[lax.rem(my_head + off, head_count)]
    logit_ref[...] = total.T

    each(0, me, lambda j: sums_copy(j, me).wait_recv())

    @pl.when(me > 0)
    def _():
        window_copy(me).wait_recv()

    sums = sums_ref[...].reshape(ck_ref.shape)
    ck_ref[...] = split(sums[:, :width])
    cv_ref[...] = split(sums[:, width:])
    loads[3].wait()
    tokens = 32

    def near(n, carry):
        start = base + rows + n * block - WINDOW_TOKENS
        k_win = kv_ref[pl.ds(pl.multiple_of(start, block), WINDOW_TOKENS + block), :width]
        v_win = kv_ref[pl.ds(pl.multiple_of(start, block), WINDOW_TOKENS + block), width:]
        v_win = jnp.concatenate([v_win, jnp.ones_like(v_win)], axis=1)
        for c in range(block // tokens):
            at = pl.ds(pl.multiple_of(n * block + c * tokens, tokens), tokens)
            result = near_and_comp(
                queries[at].reshape(tokens * heads, width),
                token_gates(logit_ref[at, :], heads, (0, 2)),
                k_win,
                v_win,
                ck_ref[...],
                cv_ref[...],
                c * tokens,
                me * blocks + n,
                heads,
                block,
            )
            near_ref[at] = result.reshape(tokens, heads, width)
        return carry

    lax.fori_loop(0, blocks, near, 0)
    each(0, me - 1, lambda j: data_copy(j, me).wait_recv())
    each(0, me, lambda j: list_copy(me, j).wait_send())
    each(me + 1, count, lambda j: sums_copy(me, j).wait_send())
    each(me + 2, count, lambda j: data_copy(me, j).wait_send())

    @pl.when(me < count - 1)
    def _():
        window_copy(me + 1).wait_send()

    for off in range(1, head_count):
        part_copy(my_head, lax.rem(my_head + off, head_count)).wait_send()


def exchange(hidden, weight, keys, values, comp_key, comp_value, lists, queries, count, head_count):
    rows, width = keys.shape
    block = comp_key.shape[0]
    blocks = rows // block
    columns = weight.shape[0] // head_count
    padded = (blocks, 128)
    per = SLOTS * block
    whole = pl.BlockSpec(memory_space=pltpu.VMEM)
    far = pl.BlockSpec(memory_space=pltpu.HBM)
    dma = pltpu.SemaphoreType.DMA
    return pl.pallas_call(
        exchange_kernel,
        out_shape=(
            jax.ShapeDtypeStruct((count * per + 2 * rows, 2 * width), BF16),
            jax.ShapeDtypeStruct(queries.shape, F32),
            jax.ShapeDtypeStruct((rows, columns), F32),
            jax.ShapeDtypeStruct(padded, jnp.int32),
        ),
        in_specs=[far, whole, far, far, whole, whole, whole, far],
        out_specs=(whole,) * 4,
        scratch_shapes=[
            pltpu.VMEM(hidden.shape, BF16),
            pltpu.VMEM(queries.shape, BF16),
            pltpu.VMEM(keys.shape, BF16),
            pltpu.VMEM(values.shape, BF16),
            pltpu.VMEM(padded, jnp.int32),
            pltpu.VMEM((count, blocks, 2 * width), F32),
            pltpu.VMEM((count * blocks, 2 * width), BF16),
            pltpu.VMEM((count * blocks, 2 * width), BF16),
            pltpu.VMEM((count,) + padded, jnp.int32),
            pltpu.VMEM((count, per, 2 * width), BF16),
            pltpu.VMEM((head_count, columns, rows), F32),
            pltpu.VMEM((head_count, columns, rows), F32),
            dma((count,)),
            dma((count,)),
            dma((count,)),
            dma((count,)),
            dma((count,)),
            dma((count,)),
            dma((head_count,)),
            dma((head_count,)),
            dma,
            dma,
            dma((4,)),
        ],
        compiler_params=pltpu.CompilerParams(
            collective_id=0, has_side_effects=True, vmem_limit_bytes=48 * 1024 * 1024
        ),
        cost_estimate=pl.CostEstimate(
            flops=3_000_000_000, bytes_accessed=6_000_000, transcendentals=5_000_000
        ),
    )(hidden, weight, keys, values, comp_key, comp_value, lists, queries)


def selected_kernel(slot_ref, q_ref, kv_ref, near_ref, logit_ref, out_ref, k_sel, v_sel):
    block, heads, width = q_ref.shape
    picked = k_sel.shape[0] // block
    num = pl.program_id(0)
    factor = LOG2E * width**-0.5
    shard = pl.num_programs(0) * block
    own_start = pl.multiple_of(kv_ref.shape[0] - shard + num * block, block)
    own_rows = kv_ref[pl.ds(own_start, block), :]
    k_sel[0:block, :] = own_rows[:, :width]
    v_sel[0:block, :width] = own_rows[:, width:]
    v_sel[0:block, width:] = jnp.ones((block, width), BF16)
    own_key = jnp.broadcast_to(own_rows[0:1, :width].astype(F32), (block, width))
    for k in range(1, picked):
        slot = slot_ref[num, k]
        keep = jnp.where(slot >= 0, 1.0, 0.0)
        start = pl.multiple_of(jnp.maximum(slot, 0) * block, block)
        rows = kv_ref[pl.ds(start, block), :].astype(F32)
        at = slice(k * block, (k + 1) * block)
        k_sel[at, :] = (jnp.where(keep > 0, rows[:, :width], own_key)).astype(BF16)
        v_sel[at, :width] = jnp.where(keep > 0, rows[:, width:], 0.0).astype(BF16)
        v_sel[at, width:] = jnp.full((block, width), keep, F32).astype(BF16)
    tokens = 64
    rows_n = tokens * heads
    for c in range(block // tokens):
        at = slice(c * tokens, (c + 1) * tokens)
        q = q_ref[at].reshape(rows_n, width)
        row = lax.broadcasted_iota(jnp.int32, (rows_n, 128), 0) // heads + c * tokens
        col = lax.broadcasted_iota(jnp.int32, (rows_n, 128), 1)
        gate = token_gates(logit_ref[at, :], heads, (1,))[0]
        d = dot_t(q, k_sel[...])
        d = jnp.concatenate(
            [jnp.where((col <= row) | (col >= block), d[:, :128], NEG), d[:, 128:]], axis=1
        )
        m = jnp.max(d, axis=1, keepdims=True)
        p = jnp.exp2((d - m) * factor).astype(BF16)
        acc = jnp.dot(p, v_sel[...], preferred_element_type=F32)
        total = near_ref[at].reshape(rows_n, width) + acc[:, :width] * (gate / acc[:, width:])
        out_ref[at] = total.astype(BF16).reshape(tokens, heads, width)


def selected(slots, queries, kv, near, logits, block, picked):
    rows, heads, width = queries.shape
    blocks_here = rows // block
    whole = pl.BlockSpec(memory_space=pltpu.VMEM)
    scalars = pl.BlockSpec(memory_space=pltpu.SMEM)
    return pl.pallas_call(
        selected_kernel,
        grid=(blocks_here,),
        out_shape=jax.ShapeDtypeStruct(queries.shape, BF16),
        in_specs=[
            scalars,
            pl.BlockSpec((block, heads, width), lambda i: (i, 0, 0)),
            whole,
            pl.BlockSpec((block, heads, width), lambda i: (i, 0, 0)),
            pl.BlockSpec((block, logits.shape[1]), lambda i: (i, 0)),
        ],
        out_specs=pl.BlockSpec((block, heads, width), lambda i: (i, 0, 0)),
        scratch_shapes=[
            pltpu.VMEM((picked * block, width), BF16),
            pltpu.VMEM((picked * block, 2 * width), BF16),
        ],
        compiler_params=pltpu.CompilerParams(vmem_limit_bytes=48 * 1024 * 1024),
        cost_estimate=pl.CostEstimate(
            flops=4_500_000_000, bytes_accessed=8_000_000, transcendentals=9_000_000
        ),
    )(slots, queries, kv, near, logits)


def body(
    hidden_in,
    gate_weight,
    encoded_queries,
    encoded_keys,
    value_tensor,
    comp_key_weight,
    comp_value_weight,
    selection,
):
    rows_here, heads_here, head_dim = encoded_queries.shape
    block_len = comp_key_weight.shape[0]
    picked = selection.shape[-1]
    kv, near, logits, slots = exchange(
        hidden_in,
        gate_weight.T,
        encoded_keys.reshape(rows_here, head_dim),
        value_tensor.reshape(rows_here, head_dim),
        comp_key_weight,
        comp_value_weight,
        selection[:, 0, :],
        encoded_queries,
        lax.axis_size("ctx"),
        lax.axis_size("head"),
    )
    return selected(slots, encoded_queries, kv, near, logits, block_len, picked)


def solution(mesh):
    return jax.shard_map(
        body,
        mesh=mesh,
        in_specs=(
            P("ctx", "head"),
            P("head", None),
            P("ctx", "head", None),
            P("ctx", "head", None),
            P("ctx", "head", None),
            P(),
            P(),
            P("ctx", "head", None),
        ),
        out_specs=P("ctx", "head", None),
        check_vma=False,
    )
```

```python
import functools

import jax
import jax.numpy as jnp
from jax import lax
from jax.experimental import pallas as pl
from jax.experimental.pallas import tpu as pltpu
from jax.sharding import PartitionSpec as P

WINDOW_TOKENS = 512
NEG = -1e30
LOG2E = 1.4426950408889634
F32 = jnp.float32
BF16 = jnp.bfloat16


def dot_t(a, b):
    return lax.dot_general(a, b, (((1,), (1,)), ((), ())), preferred_element_type=F32)


def split(value):
    high = value.astype(BF16)
    return jnp.concatenate([high, (value - high.astype(F32)).astype(BF16)], axis=1)


def token_gates(logits, heads, wanted):
    tokens, columns = logits.shape
    gates = jax.nn.sigmoid(logits)
    gates = jnp.broadcast_to(gates[:, None, :], (tokens, heads, columns))
    gates = gates.reshape(tokens * heads, columns)
    head = lax.broadcasted_iota(jnp.int32, gates.shape, 0) % heads
    branch = lax.broadcasted_iota(jnp.int32, gates.shape, 1) - 3 * head
    return [
        jnp.sum(jnp.where(branch == b, gates, 0.0), axis=1, keepdims=True) for b in wanted
    ]


def near_and_comp(q, gates, k_win, v_win, ck, cv, first_token, own_block, heads, block):
    rows_n, width = q.shape
    window = WINDOW_TOKENS
    factor = LOG2E * width**-0.5
    comp_n = ck.shape[0]
    row = lax.broadcasted_iota(jnp.int32, (rows_n, 128), 0) // heads + first_token
    col = lax.broadcasted_iota(jnp.int32, (rows_n, 128), 1)
    d = dot_t(q, k_win)
    low = window - own_block * block
    wcol = lax.broadcasted_iota(jnp.int32, (1, window - 128), 1) + 128
    head_part = jnp.where((col > row) & (col >= low), d[:, :128], NEG)
    mid_part = d[:, 128:window] + jnp.where(wcol >= low, 0.0, NEG)
    own_part = jnp.where(col[:, :block] <= row[:, :block], d[:, window:], NEG)
    d = jnp.concatenate([head_part, mid_part, own_part], axis=1)
    m = jnp.max(d, axis=1, keepdims=True)
    p = jnp.exp2((d - m) * factor).astype(BF16)
    acc = jnp.dot(p, v_win, preferred_element_type=F32)
    total = acc[:, :width] * (gates[1] / acc[:, width:])
    d = dot_t(jnp.concatenate([q, q], axis=1), ck)
    crow = lax.broadcasted_iota(jnp.int32, (rows_n, comp_n), 0) // heads + first_token
    ccol = lax.broadcasted_iota(jnp.int32, (rows_n, comp_n), 1)
    d = jnp.where((ccol + 1) * block - 1 <= crow + own_block * block, d, NEG)
    m = jnp.maximum(jnp.max(d, axis=1, keepdims=True), 0.0)
    p = jnp.exp2((d - m) * factor)
    sums = jnp.sum(p, axis=1, keepdims=True) + jnp.exp2(-m * factor)
    acc = jnp.dot(p.astype(BF16), cv, preferred_element_type=F32)
    return total + (acc[:, :width] + acc[:, width:]) * (gates[0] / sums)


SLOTS = 4
VMEM_BYTES = 62 * 1024 * 1024
MESH = pl.DeviceIdType.MESH


def exchange_kernel(
    hidden_ref,
    weight_ref,
    key_ref,
    value_ref,
    comp_key_ref,
    comp_value_ref,
    short_ref,
    query_ref,
    kv_ref,
    near_ref,
    logit_ref,
    slot_ref,
    hidden,
    queries,
    keys,
    values,
    sel_ref,
    sums_ref,
    ck_ref,
    cv_ref,
    lists,
    stage,
    partial,
    parts,
    list_send,
    list_recv,
    data_send,
    data_recv,
    sums_send,
    sums_recv,
    part_send,
    part_recv,
    win_send,
    win_recv,
    load_sem,
    near_buf,
    near_sem,
):
    count = lax.axis_size("ctx")
    head_count = lax.axis_size("head")
    me = lax.axis_index("ctx")
    my_head = lax.axis_index("head")
    rows, width = key_ref.shape
    block = comp_key_ref.shape[0]
    heads = query_ref.shape[1]
    blocks = rows // block
    per = SLOTS * block
    base = count * per
    columns = logit_ref.shape[1]

    loads = [
        pltpu.make_async_copy(source, target, load_sem.at[n])
        for n, (source, target) in enumerate(
            ((key_ref, keys), (value_ref, values), (hidden_ref, hidden), (query_ref, queries))
        )
    ]
    for load in loads:
        load.start()
    barrier = pltpu.get_barrier_semaphore()

    def greet(off, carry):
        pl.semaphore_signal(
            barrier, inc=1, device_id={"ctx": lax.rem(me + off, count)}, device_id_type=MESH
        )
        return carry

    lax.fori_loop(1, count, greet, 0)
    for off in range(1, head_count):
        pl.semaphore_signal(
            barrier,
            inc=1,
            device_id={"head": lax.rem(my_head + off, head_count)},
            device_id_type=MESH,
        )
    short = short_ref[...]
    sel_ref[...] = jnp.full(sel_ref.shape, -1, jnp.int32)
    sel_ref[:, : short.shape[1]] = short
    loads[0].wait()
    loads[1].wait()
    kv_ref[pl.ds(base + rows, rows), :width] = keys[...]
    kv_ref[pl.ds(base + rows, rows), width:] = values[...]
    comp_weights = jnp.concatenate([comp_key_ref[...], comp_value_ref[...]], axis=1)
    summary = jnp.concatenate(
        [
            jnp.sum(
                kv_ref[base + rows + n * block : base + rows + (n + 1) * block, :].astype(F32)
                * comp_weights,
                axis=0,
                keepdims=True,
            )
            for n in range(blocks)
        ],
        axis=0,
    )
    sums_ref[me] = summary

    @pl.when(me == 0)
    def _():
        kv_ref[base : base + rows, :] = jnp.zeros((rows, 2 * width), BF16)

    def clear(j, carry):
        sums_ref[j] = jnp.zeros(summary.shape, F32)
        return carry

    lax.fori_loop(me + 1, count, clear, 0)
    pl.semaphore_wait(barrier, count - 1 + head_count - 1)

    def list_copy(source, target):
        return pltpu.make_async_remote_copy(
            src_ref=sel_ref,
            dst_ref=lists.at[source],
            send_sem=list_send.at[target],
            recv_sem=list_recv.at[source],
            device_id={"ctx": target},
            device_id_type=MESH,
        )

    def sums_copy(source, target):
        return pltpu.make_async_remote_copy(
            src_ref=sums_ref.at[source],
            dst_ref=sums_ref.at[source],
            send_sem=sums_send.at[target],
            recv_sem=sums_recv.at[source],
            device_id={"ctx": target},
            device_id_type=MESH,
        )

    def data_copy(source, target):
        return pltpu.make_async_remote_copy(
            src_ref=stage.at[target],
            dst_ref=kv_ref.at[pl.ds(pl.multiple_of(source * per, per), per)],
            send_sem=data_send.at[target],
            recv_sem=data_recv.at[source],
            device_id={"ctx": target},
            device_id_type=MESH,
        )

    def window_copy(target):
        return pltpu.make_async_remote_copy(
            src_ref=kv_ref.at[pl.ds(base + rows, rows)],
            dst_ref=kv_ref.at[pl.ds(base, rows)],
            send_sem=win_send,
            recv_sem=win_recv,
            device_id={"ctx": target},
            device_id_type=MESH,
        )

    def part_copy(source, target):
        return pltpu.make_async_remote_copy(
            src_ref=partial.at[target],
            dst_ref=parts.at[source],
            send_sem=part_send.at[target],
            recv_sem=part_recv.at[source],
            device_id={"head": target},
            device_id_type=MESH,
        )

    def each(first, last, step):
        def run(j, carry):
            step(j)
            return carry

        lax.fori_loop(first, last, run, 0)

    each(0, me, lambda j: list_copy(me, j).start())

    @pl.when(me < count - 1)
    def _():
        window_copy(me + 1).start()

    each(me + 1, count, lambda j: sums_copy(me, j).start())

    loads[2].wait()
    logits = dot_t(weight_ref[...], hidden[...])
    for h in range(head_count):
        partial[h] = logits[h * columns : (h + 1) * columns, :]
    for off in range(1, head_count):
        part_copy(my_head, lax.rem(my_head + off, head_count)).start()

    def pack(step, carry):
        target = count - 1 - step
        list_copy(target, me).wait_recv()
        wanted = lists[target]
        rank = jnp.zeros((1, 1), F32)
        places = []
        for n in range(blocks):
            need = jnp.max(
                jnp.where(wanted == me * blocks + n, 1.0, 0.0), axis=(0, 1), keepdims=True
            )
            places.append(jnp.where(need > 0, rank, -1.0))
            rank = rank + need
        for s in range(SLOTS):
            packed = jnp.zeros((block, 2 * width), F32)
            for n in range(blocks):
                rows_n = kv_ref[base + rows + n * block : base + rows + (n + 1) * block, :]
                packed = jnp.where(places[n] == s, rows_n.astype(F32), packed)
            stage[target, s * block : (s + 1) * block, :] = packed.astype(BF16)
        return carry

    lax.fori_loop(0, count - 2 - me, pack, 0)

    @pl.when(me > 0)
    def _():
        window_copy(me).wait_recv()

    @pl.when(me < count - 1)
    def _():
        list_copy(me + 1, me).wait_recv()
        window_copy(me + 1).wait_send()

    def send(step, carry):
        data_copy(me, count - 1 - step).start()
        return carry

    lax.fori_loop(0, count - 2 - me, send, 0)

    mine = sel_ref[...]
    query = lax.broadcasted_iota(jnp.int32, mine.shape, 0) + me * blocks

    def place(j, slots):
        rank = jnp.zeros((1, 1), F32)
        for n in range(blocks):
            named = mine == j * blocks + n
            need = jnp.max(jnp.where(named, 1.0, 0.0), axis=(0, 1), keepdims=True)
            packed = rank.astype(jnp.int32) + j * SLOTS
            whole = count * SLOTS + n + (j - me + 1) * blocks
            place_n = jnp.where(j < me - 1, packed, whole)
            slots = jnp.where(named & (j * blocks + n <= query), place_n, slots)
            rank = rank + need
        return slots

    slot_ref[...] = lax.fori_loop(0, me + 1, place, jnp.full(mine.shape, -1, jnp.int32))

    for off in range(1, head_count):
        part_copy(lax.rem(my_head + off, head_count), my_head).wait_recv()
    total = partial[my_head]
    for off in range(1, head_count):
        total += parts[lax.rem(my_head + off, head_count)]
    logit_ref[...] = total.T

    each(0, me, lambda j: sums_copy(j, me).wait_recv())
    sums = sums_ref[...].reshape(ck_ref.shape)
    ck_ref[...] = split(sums[:, :width])
    cv_ref[...] = split(sums[:, width:])
    loads[3].wait()
    tokens = 32

    def near_copy(n):
        at = pl.ds(pl.multiple_of(n * block, block), block)
        return pltpu.make_async_copy(near_buf.at[at], near_ref.at[at], near_sem.at[n])

    def near(n, carry):
        start = base + rows + n * block - WINDOW_TOKENS
        k_win = kv_ref[pl.ds(pl.multiple_of(start, block), WINDOW_TOKENS + block), :width]
        v_win = kv_ref[pl.ds(pl.multiple_of(start, block), WINDOW_TOKENS + block), width:]
        v_win = jnp.concatenate([v_win, jnp.ones_like(v_win)], axis=1)
        for c in range(block // tokens):
            at = pl.ds(pl.multiple_of(n * block + c * tokens, tokens), tokens)
            result = near_and_comp(
                queries[at].reshape(tokens * heads, width),
                token_gates(logit_ref[at, :], heads, (0, 2)),
                k_win,
                v_win,
                ck_ref[...],
                cv_ref[...],
                c * tokens,
                me * blocks + n,
                heads,
                block,
            )
            near_buf[at] = result.reshape(tokens, heads, width)
        near_copy(n).start()
        return carry

    lax.fori_loop(0, blocks, near, 0)
    each(0, me - 1, lambda j: data_copy(j, me).wait_recv())
    each(0, me, lambda j: list_copy(me, j).wait_send())
    each(me + 1, count, lambda j: sums_copy(me, j).wait_send())
    each(me + 2, count, lambda j: data_copy(me, j).wait_send())
    each(0, blocks, lambda n: near_copy(n).wait())

    for off in range(1, head_count):
        part_copy(my_head, lax.rem(my_head + off, head_count)).wait_send()


def exchange(hidden, weight, keys, values, comp_key, comp_value, lists, queries, count, head_count):
    rows, width = keys.shape
    block = comp_key.shape[0]
    blocks = rows // block
    columns = weight.shape[0] // head_count
    padded = (blocks, 128)
    per = SLOTS * block
    whole = pl.BlockSpec(memory_space=pltpu.VMEM)
    far = pl.BlockSpec(memory_space=pltpu.HBM)
    dma = pltpu.SemaphoreType.DMA
    return pl.pallas_call(
        exchange_kernel,
        out_shape=(
            jax.ShapeDtypeStruct((count * per + 2 * rows, 2 * width), BF16),
            jax.ShapeDtypeStruct(queries.shape, F32),
            jax.ShapeDtypeStruct((rows, columns), F32),
            jax.ShapeDtypeStruct(padded, jnp.int32),
        ),
        in_specs=[far, whole, far, far, whole, whole, whole, far],
        out_specs=(whole, far, whole, whole),
        scratch_shapes=[
            pltpu.VMEM(hidden.shape, BF16),
            pltpu.VMEM(queries.shape, BF16),
            pltpu.VMEM(keys.shape, BF16),
            pltpu.VMEM(values.shape, BF16),
            pltpu.VMEM(padded, jnp.int32),
            pltpu.VMEM((count, blocks, 2 * width), F32),
            pltpu.VMEM((count * blocks, 2 * width), BF16),
            pltpu.VMEM((count * blocks, 2 * width), BF16),
            pltpu.VMEM((count,) + padded, jnp.int32),
            pltpu.VMEM((count, per, 2 * width), BF16),
            pltpu.VMEM((head_count, columns, rows), F32),
            pltpu.VMEM((head_count, columns, rows), F32),
            dma((count,)),
            dma((count,)),
            dma((count,)),
            dma((count,)),
            dma((count,)),
            dma((count,)),
            dma((head_count,)),
            dma((head_count,)),
            dma,
            dma,
            dma((4,)),
            pltpu.VMEM(queries.shape, F32),
            dma((blocks,)),
        ],
        compiler_params=pltpu.CompilerParams(
            collective_id=0, has_side_effects=True, vmem_limit_bytes=VMEM_BYTES
        ),
        cost_estimate=pl.CostEstimate(
            flops=3_000_000_000, bytes_accessed=6_000_000, transcendentals=5_000_000
        ),
    )(hidden, weight, keys, values, comp_key, comp_value, lists, queries)


def selected_kernel(slot_ref, q_ref, kv_ref, near_ref, logit_ref, out_ref, k_sel, v_sel):
    block, heads, width = q_ref.shape
    picked = k_sel.shape[0] // block
    num = pl.program_id(0)
    factor = LOG2E * width**-0.5
    shard = pl.num_programs(0) * block
    own_start = pl.multiple_of(kv_ref.shape[0] - shard + num * block, block)
    own_rows = kv_ref[pl.ds(own_start, block), :]
    k_sel[0:block, :] = own_rows[:, :width]
    v_sel[0:block, :width] = own_rows[:, width:]
    v_sel[0:block, width:] = jnp.ones((block, width), BF16)
    own_key = jnp.broadcast_to(own_rows[0:1, :width].astype(F32), (block, width)).astype(BF16)
    for k in range(1, picked):
        slot = slot_ref[num, k]
        keep = jnp.full((block, width), jnp.where(slot >= 0, 1.0, 0.0), F32).astype(BF16)
        start = pl.multiple_of(jnp.where(slot >= 0, slot * block, own_start), block)
        rows = kv_ref[pl.ds(start, block), :]
        at = slice(k * block, (k + 1) * block)
        k_sel[at, :] = rows[:, :width] * keep + own_key * (1.0 - keep)
        v_sel[at, :width] = rows[:, width:] * keep
        v_sel[at, width:] = keep
    tokens = 32
    rows_n = tokens * heads
    for c in range(block // tokens):
        at = slice(c * tokens, (c + 1) * tokens)
        q = q_ref[at].reshape(rows_n, width)
        row = lax.broadcasted_iota(jnp.int32, (rows_n, 128), 0) // heads + c * tokens
        col = lax.broadcasted_iota(jnp.int32, (rows_n, 128), 1)
        gate = token_gates(logit_ref[at, :], heads, (1,))[0]
        d = dot_t(q, k_sel[...])
        d = jnp.concatenate(
            [jnp.where((col <= row) | (col >= block), d[:, :128], NEG), d[:, 128:]], axis=1
        )
        m = jnp.max(d, axis=1, keepdims=True)
        p = jnp.exp2((d - m) * factor).astype(BF16)
        acc = jnp.dot(p, v_sel[...], preferred_element_type=F32)
        total = near_ref[at].reshape(rows_n, width) + acc[:, :width] * (gate / acc[:, width:])
        out_ref[at] = total.astype(BF16).reshape(tokens, heads, width)


def selected(slots, queries, kv, near, logits, block, picked):
    rows, heads, width = queries.shape
    blocks_here = rows // block
    whole = pl.BlockSpec(memory_space=pltpu.VMEM)
    scalars = pl.BlockSpec(memory_space=pltpu.SMEM)
    return pl.pallas_call(
        selected_kernel,
        grid=(blocks_here,),
        out_shape=jax.ShapeDtypeStruct(queries.shape, BF16),
        in_specs=[
            scalars,
            pl.BlockSpec((block, heads, width), lambda i: (i, 0, 0)),
            whole,
            pl.BlockSpec((block, heads, width), lambda i: (i, 0, 0)),
            pl.BlockSpec((block, logits.shape[1]), lambda i: (i, 0)),
        ],
        out_specs=pl.BlockSpec((block, heads, width), lambda i: (i, 0, 0)),
        scratch_shapes=[
            pltpu.VMEM((picked * block, width), BF16),
            pltpu.VMEM((picked * block, 2 * width), BF16),
        ],
        compiler_params=pltpu.CompilerParams(vmem_limit_bytes=VMEM_BYTES),
        cost_estimate=pl.CostEstimate(
            flops=4_500_000_000, bytes_accessed=8_000_000, transcendentals=9_000_000
        ),
    )(slots, queries, kv, near, logits)


def body(
    hidden_in,
    gate_weight,
    encoded_queries,
    encoded_keys,
    value_tensor,
    comp_key_weight,
    comp_value_weight,
    selection,
):
    rows_here, heads_here, head_dim = encoded_queries.shape
    block_len = comp_key_weight.shape[0]
    picked = selection.shape[-1]
    kv, near, logits, slots = exchange(
        hidden_in,
        gate_weight.T,
        encoded_keys.reshape(rows_here, head_dim),
        value_tensor.reshape(rows_here, head_dim),
        comp_key_weight,
        comp_value_weight,
        selection[:, 0, :],
        encoded_queries,
        lax.axis_size("ctx"),
        lax.axis_size("head"),
    )
    return selected(slots, encoded_queries, kv, near, logits, block_len, picked)


def solution(mesh):
    return jax.shard_map(
        body,
        mesh=mesh,
        in_specs=(
            P("ctx", "head"),
            P("head", None),
            P("ctx", "head", None),
            P("ctx", "head", None),
            P("ctx", "head", None),
            P(),
            P(),
            P("ctx", "head", None),
        ),
        out_specs=P("ctx", "head", None),
        check_vma=False,
    )
```

```python
import functools

import jax
import jax.numpy as jnp
from jax import lax
from jax.experimental import pallas as pl
from jax.experimental.pallas import tpu as pltpu
from jax.sharding import PartitionSpec as P

WINDOW_TOKENS = 512
NEG = -1e30
LOG2E = 1.4426950408889634
F32 = jnp.float32
BF16 = jnp.bfloat16


def dot_t(a, b):
    return lax.dot_general(a, b, (((1,), (1,)), ((), ())), preferred_element_type=F32)


def split(value):
    high = value.astype(BF16)
    return jnp.concatenate([high, (value - high.astype(F32)).astype(BF16)], axis=1)


def token_gates(logits, heads, wanted):
    tokens, columns = logits.shape
    gates = jax.nn.sigmoid(logits)
    gates = jnp.broadcast_to(gates[:, None, :], (tokens, heads, columns))
    gates = gates.reshape(tokens * heads, columns)
    head = lax.broadcasted_iota(jnp.int32, gates.shape, 0) % heads
    branch = lax.broadcasted_iota(jnp.int32, gates.shape, 1) - 3 * head
    return [
        jnp.sum(jnp.where(branch == b, gates, 0.0), axis=1, keepdims=True) for b in wanted
    ]


def near_and_comp(q, gates, k_win, v_win, ck, cv, first_token, own_block, heads, block):
    rows_n, width = q.shape
    window = WINDOW_TOKENS
    factor = LOG2E * width**-0.5
    comp_n = ck.shape[0]
    row = lax.broadcasted_iota(jnp.int32, (rows_n, 128), 0) // heads + first_token
    col = lax.broadcasted_iota(jnp.int32, (rows_n, 128), 1)
    d = dot_t(q, k_win)
    low = window - own_block * block
    wcol = lax.broadcasted_iota(jnp.int32, (1, window - 128), 1) + 128
    head_part = jnp.where((col > row) & (col >= low), d[:, :128], NEG)
    mid_part = d[:, 128:window] + jnp.where(wcol >= low, 0.0, NEG)
    own_part = jnp.where(col[:, :block] <= row[:, :block], d[:, window:], NEG)
    d = jnp.concatenate([head_part, mid_part, own_part], axis=1)
    m = jnp.max(d, axis=1, keepdims=True)
    p = jnp.exp2((d - m) * factor).astype(BF16)
    acc = jnp.dot(p, v_win, preferred_element_type=F32)
    total = acc[:, :width] * (gates[1] / acc[:, width:])
    d = dot_t(jnp.concatenate([q, q], axis=1), ck)
    crow = lax.broadcasted_iota(jnp.int32, (rows_n, comp_n), 0) // heads + first_token
    ccol = lax.broadcasted_iota(jnp.int32, (rows_n, comp_n), 1)
    d = jnp.where((ccol + 1) * block - 1 <= crow + own_block * block, d, NEG)
    m = jnp.maximum(jnp.max(d, axis=1, keepdims=True), 0.0)
    p = jnp.exp2((d - m) * factor)
    sums = jnp.sum(p, axis=1, keepdims=True) + jnp.exp2(-m * factor)
    acc = jnp.dot(p.astype(BF16), cv, preferred_element_type=F32)
    return total + (acc[:, :width] + acc[:, width:]) * (gates[0] / sums)


SLOTS = 4
VMEM_BYTES = 62 * 1024 * 1024
MESH = pl.DeviceIdType.MESH


def exchange_kernel(
    hidden_ref,
    weight_ref,
    key_ref,
    value_ref,
    comp_key_ref,
    comp_value_ref,
    short_ref,
    query_ref,
    kv_ref,
    near_ref,
    logit_ref,
    slot_ref,
    hidden,
    queries,
    keys,
    values,
    sel_ref,
    sums_ref,
    ck_ref,
    cv_ref,
    lists,
    stage,
    partial,
    parts,
    list_send,
    list_recv,
    data_send,
    data_recv,
    sums_send,
    sums_recv,
    part_send,
    part_recv,
    win_send,
    win_recv,
    load_sem,
    near_buf,
    near_sem,
):
    count = lax.axis_size("ctx")
    head_count = lax.axis_size("head")
    me = lax.axis_index("ctx")
    my_head = lax.axis_index("head")
    rows, width = key_ref.shape
    block = comp_key_ref.shape[0]
    heads = query_ref.shape[1]
    blocks = rows // block
    per = SLOTS * block
    base = count * per
    columns = logit_ref.shape[1]

    loads = [
        pltpu.make_async_copy(source, target, load_sem.at[n])
        for n, (source, target) in enumerate(
            ((key_ref, keys), (value_ref, values), (hidden_ref, hidden), (query_ref, queries))
        )
    ]
    for load in loads:
        load.start()
    barrier = pltpu.get_barrier_semaphore()

    def greet(off, carry):
        pl.semaphore_signal(
            barrier, inc=1, device_id={"ctx": lax.rem(me + off, count)}, device_id_type=MESH
        )
        return carry

    lax.fori_loop(1, count, greet, 0)
    for off in range(1, head_count):
        pl.semaphore_signal(
            barrier,
            inc=1,
            device_id={"head": lax.rem(my_head + off, head_count)},
            device_id_type=MESH,
        )
    short = short_ref[...]
    sel_ref[...] = jnp.full(sel_ref.shape, -1, jnp.int32)
    sel_ref[:, : short.shape[1]] = short
    loads[0].wait()
    loads[1].wait()
    kv_ref[pl.ds(base + rows, rows), :width] = keys[...]
    kv_ref[pl.ds(base + rows, rows), width:] = values[...]
    comp_weights = jnp.concatenate([comp_key_ref[...], comp_value_ref[...]], axis=1)
    summary = jnp.concatenate(
        [
            jnp.sum(
                kv_ref[base + rows + n * block : base + rows + (n + 1) * block, :].astype(F32)
                * comp_weights,
                axis=0,
                keepdims=True,
            )
            for n in range(blocks)
        ],
        axis=0,
    )
    sums_ref[me] = summary

    @pl.when(me == 0)
    def _():
        kv_ref[base : base + rows, :] = jnp.zeros((rows, 2 * width), BF16)

    def clear(j, carry):
        sums_ref[j] = jnp.zeros(summary.shape, F32)
        return carry

    lax.fori_loop(me + 1, count, clear, 0)
    pl.semaphore_wait(barrier, count - 1 + head_count - 1)

    def list_copy(source, target):
        return pltpu.make_async_remote_copy(
            src_ref=sel_ref,
            dst_ref=lists.at[source],
            send_sem=list_send.at[target],
            recv_sem=list_recv.at[source],
            device_id={"ctx": target},
            device_id_type=MESH,
        )

    def sums_copy(source, target):
        return pltpu.make_async_remote_copy(
            src_ref=sums_ref.at[source],
            dst_ref=sums_ref.at[source],
            send_sem=sums_send.at[target],
            recv_sem=sums_recv.at[source],
            device_id={"ctx": target},
            device_id_type=MESH,
        )

    def data_copy(source, target):
        return pltpu.make_async_remote_copy(
            src_ref=stage.at[target],
            dst_ref=kv_ref.at[pl.ds(pl.multiple_of(source * per, per), per)],
            send_sem=data_send.at[target],
            recv_sem=data_recv.at[source],
            device_id={"ctx": target},
            device_id_type=MESH,
        )

    def window_copy(target):
        return pltpu.make_async_remote_copy(
            src_ref=kv_ref.at[pl.ds(base + rows, rows)],
            dst_ref=kv_ref.at[pl.ds(base, rows)],
            send_sem=win_send,
            recv_sem=win_recv,
            device_id={"ctx": target},
            device_id_type=MESH,
        )

    def part_copy(source, target):
        return pltpu.make_async_remote_copy(
            src_ref=partial.at[target],
            dst_ref=parts.at[source],
            send_sem=part_send.at[target],
            recv_sem=part_recv.at[source],
            device_id={"head": target},
            device_id_type=MESH,
        )

    def each(first, last, step):
        def run(j, carry):
            step(j)
            return carry

        lax.fori_loop(first, last, run, 0)

    each(0, me, lambda j: list_copy(me, j).start())

    @pl.when(me < count - 1)
    def _():
        window_copy(me + 1).start()

    each(me + 1, count, lambda j: sums_copy(me, j).start())

    def pack(step, carry):
        target = count - 1 - step
        list_copy(target, me).wait_recv()
        wanted = lists[target]
        rank = jnp.zeros((1, 1), F32)
        places = []
        for n in range(blocks):
            need = jnp.max(
                jnp.where(wanted == me * blocks + n, 1.0, 0.0), axis=(0, 1), keepdims=True
            )
            places.append(jnp.where(need > 0, rank, -1.0))
            rank = rank + need
        for s in range(SLOTS):
            packed = jnp.zeros((block, 2 * width), BF16)
            for n in range(blocks):
                rows_n = kv_ref[base + rows + n * block : base + rows + (n + 1) * block, :]
                chosen = jnp.where(places[n] == s, 1.0, 0.0)
                packed += rows_n * jnp.broadcast_to(chosen, rows_n.shape).astype(BF16)
            stage[target, s * block : (s + 1) * block, :] = packed
        return carry

    lax.fori_loop(0, count - 2 - me, pack, 0)

    @pl.when(me < count - 1)
    def _():
        list_copy(me + 1, me).wait_recv()
        window_copy(me + 1).wait_send()

    def send(step, carry):
        data_copy(me, count - 1 - step).start()
        return carry

    lax.fori_loop(0, count - 2 - me, send, 0)

    loads[2].wait()
    logits = dot_t(weight_ref[...], hidden[...])
    for h in range(head_count):
        partial[h] = logits[h * columns : (h + 1) * columns, :]
    for off in range(1, head_count):
        part_copy(my_head, lax.rem(my_head + off, head_count)).start()

    mine = sel_ref[...]
    query = lax.broadcasted_iota(jnp.int32, mine.shape, 0) + me * blocks

    def place(j, slots):
        rank = jnp.zeros((1, 1), F32)
        for n in range(blocks):
            named = mine == j * blocks + n
            need = jnp.max(jnp.where(named, 1.0, 0.0), axis=(0, 1), keepdims=True)
            packed = rank.astype(jnp.int32) + j * SLOTS
            whole = count * SLOTS + n + (j - me + 1) * blocks
            place_n = jnp.where(j < me - 1, packed, whole)
            slots = jnp.where(named & (j * blocks + n <= query), place_n, slots)
            rank = rank + need
        return slots

    slot_ref[...] = lax.fori_loop(0, me + 1, place, jnp.full(mine.shape, -1, jnp.int32))

    for off in range(1, head_count):
        part_copy(lax.rem(my_head + off, head_count), my_head).wait_recv()
    total = partial[my_head]
    for off in range(1, head_count):
        total += parts[lax.rem(my_head + off, head_count)]
    logit_ref[...] = total.T

    each(0, me, lambda j: sums_copy(j, me).wait_recv())
    @pl.when(me > 0)
    def _():
        window_copy(me).wait_recv()

    sums = sums_ref[...].reshape(ck_ref.shape)
    ck_ref[...] = split(sums[:, :width])
    cv_ref[...] = split(sums[:, width:])
    loads[3].wait()
    tokens = 32

    def near_copy(n):
        at = pl.ds(pl.multiple_of(n * block, block), block)
        return pltpu.make_async_copy(near_buf.at[at], near_ref.at[at], near_sem.at[n])

    def near(n, carry):
        start = base + rows + n * block - WINDOW_TOKENS
        k_win = kv_ref[pl.ds(pl.multiple_of(start, block), WINDOW_TOKENS + block), :width]
        v_win = kv_ref[pl.ds(pl.multiple_of(start, block), WINDOW_TOKENS + block), width:]
        v_win = jnp.concatenate([v_win, jnp.ones_like(v_win)], axis=1)
        for c in range(block // tokens):
            at = pl.ds(pl.multiple_of(n * block + c * tokens, tokens), tokens)
            result = near_and_comp(
                queries[at].reshape(tokens * heads, width),
                token_gates(logit_ref[at, :], heads, (0, 2)),
                k_win,
                v_win,
                ck_ref[...],
                cv_ref[...],
                c * tokens,
                me * blocks + n,
                heads,
                block,
            )
            near_buf[at] = result.reshape(tokens, heads, width)
        near_copy(n).start()
        return carry

    lax.fori_loop(0, blocks, near, 0)
    each(0, me - 1, lambda j: data_copy(j, me).wait_recv())
    each(0, me, lambda j: list_copy(me, j).wait_send())
    each(me + 1, count, lambda j: sums_copy(me, j).wait_send())
    each(me + 2, count, lambda j: data_copy(me, j).wait_send())
    each(0, blocks, lambda n: near_copy(n).wait())

    for off in range(1, head_count):
        part_copy(my_head, lax.rem(my_head + off, head_count)).wait_send()


def exchange(hidden, weight, keys, values, comp_key, comp_value, lists, queries, count, head_count):
    rows, width = keys.shape
    block = comp_key.shape[0]
    blocks = rows // block
    columns = weight.shape[0] // head_count
    padded = (blocks, 128)
    per = SLOTS * block
    whole = pl.BlockSpec(memory_space=pltpu.VMEM)
    far = pl.BlockSpec(memory_space=pltpu.HBM)
    dma = pltpu.SemaphoreType.DMA
    return pl.pallas_call(
        exchange_kernel,
        out_shape=(
            jax.ShapeDtypeStruct((count * per + 2 * rows, 2 * width), BF16),
            jax.ShapeDtypeStruct(queries.shape, F32),
            jax.ShapeDtypeStruct((rows, columns), F32),
            jax.ShapeDtypeStruct(padded, jnp.int32),
        ),
        in_specs=[far, whole, far, far, whole, whole, whole, far],
        out_specs=(whole, far, whole, whole),
        scratch_shapes=[
            pltpu.VMEM(hidden.shape, BF16),
            pltpu.VMEM(queries.shape, BF16),
            pltpu.VMEM(keys.shape, BF16),
            pltpu.VMEM(values.shape, BF16),
            pltpu.VMEM(padded, jnp.int32),
            pltpu.VMEM((count, blocks, 2 * width), F32),
            pltpu.VMEM((count * blocks, 2 * width), BF16),
            pltpu.VMEM((count * blocks, 2 * width), BF16),
            pltpu.VMEM((count,) + padded, jnp.int32),
            pltpu.VMEM((count, per, 2 * width), BF16),
            pltpu.VMEM((head_count, columns, rows), F32),
            pltpu.VMEM((head_count, columns, rows), F32),
            dma((count,)),
            dma((count,)),
            dma((count,)),
            dma((count,)),
            dma((count,)),
            dma((count,)),
            dma((head_count,)),
            dma((head_count,)),
            dma,
            dma,
            dma((4,)),
            pltpu.VMEM(queries.shape, F32),
            dma((blocks,)),
        ],
        compiler_params=pltpu.CompilerParams(
            collective_id=0, has_side_effects=True, vmem_limit_bytes=VMEM_BYTES
        ),
        cost_estimate=pl.CostEstimate(
            flops=3_000_000_000, bytes_accessed=6_000_000, transcendentals=5_000_000
        ),
    )(hidden, weight, keys, values, comp_key, comp_value, lists, queries)


def selected_kernel(slot_ref, q_ref, kv_ref, near_ref, logit_ref, out_ref, k_sel, v_sel):
    block, heads, width = q_ref.shape
    picked = k_sel.shape[0] // block
    num = pl.program_id(0)
    factor = LOG2E * width**-0.5
    shard = pl.num_programs(0) * block
    own_start = pl.multiple_of(kv_ref.shape[0] - shard + num * block, block)
    own_rows = kv_ref[pl.ds(own_start, block), :]
    k_sel[0:block, :] = own_rows[:, :width]
    v_sel[0:block, :width] = own_rows[:, width:]
    v_sel[0:block, width:] = jnp.ones((block, width), BF16)
    own_key = jnp.broadcast_to(own_rows[0:1, :width].astype(F32), (block, width)).astype(BF16)
    for k in range(1, picked):
        slot = slot_ref[num, k]
        keep = jnp.full((block, width), jnp.where(slot >= 0, 1.0, 0.0), F32).astype(BF16)
        start = pl.multiple_of(jnp.where(slot >= 0, slot * block, own_start), block)
        rows = kv_ref[pl.ds(start, block), :]
        at = slice(k * block, (k + 1) * block)
        k_sel[at, :] = rows[:, :width] * keep + own_key * (1.0 - keep)
        v_sel[at, :width] = rows[:, width:] * keep
        v_sel[at, width:] = keep
    tokens = 32
    rows_n = tokens * heads
    for c in range(block // tokens):
        at = slice(c * tokens, (c + 1) * tokens)
        q = q_ref[at].reshape(rows_n, width)
        row = lax.broadcasted_iota(jnp.int32, (rows_n, 128), 0) // heads + c * tokens
        col = lax.broadcasted_iota(jnp.int32, (rows_n, 128), 1)
        gate = token_gates(logit_ref[at, :], heads, (1,))[0]
        d = dot_t(q, k_sel[...])
        d = jnp.concatenate(
            [jnp.where((col <= row) | (col >= block), d[:, :128], NEG), d[:, 128:]], axis=1
        )
        m = jnp.max(d, axis=1, keepdims=True)
        p = jnp.exp2((d - m) * factor).astype(BF16)
        acc = jnp.dot(p, v_sel[...], preferred_element_type=F32)
        total = near_ref[at].reshape(rows_n, width) + acc[:, :width] * (gate / acc[:, width:])
        out_ref[at] = total.astype(BF16).reshape(tokens, heads, width)


def selected(slots, queries, kv, near, logits, block, picked):
    rows, heads, width = queries.shape
    blocks_here = rows // block
    whole = pl.BlockSpec(memory_space=pltpu.VMEM)
    scalars = pl.BlockSpec(memory_space=pltpu.SMEM)
    return pl.pallas_call(
        selected_kernel,
        grid=(blocks_here,),
        out_shape=jax.ShapeDtypeStruct(queries.shape, BF16),
        in_specs=[
            scalars,
            pl.BlockSpec((block, heads, width), lambda i: (i, 0, 0)),
            whole,
            pl.BlockSpec((block, heads, width), lambda i: (i, 0, 0)),
            pl.BlockSpec((block, logits.shape[1]), lambda i: (i, 0)),
        ],
        out_specs=pl.BlockSpec((block, heads, width), lambda i: (i, 0, 0)),
        scratch_shapes=[
            pltpu.VMEM((picked * block, width), BF16),
            pltpu.VMEM((picked * block, 2 * width), BF16),
        ],
        compiler_params=pltpu.CompilerParams(vmem_limit_bytes=VMEM_BYTES),
        cost_estimate=pl.CostEstimate(
            flops=4_500_000_000, bytes_accessed=8_000_000, transcendentals=9_000_000
        ),
    )(slots, queries, kv, near, logits)


def body(
    hidden_in,
    gate_weight,
    encoded_queries,
    encoded_keys,
    value_tensor,
    comp_key_weight,
    comp_value_weight,
    selection,
):
    rows_here, heads_here, head_dim = encoded_queries.shape
    block_len = comp_key_weight.shape[0]
    picked = selection.shape[-1]
    kv, near, logits, slots = exchange(
        hidden_in,
        gate_weight.T,
        encoded_keys.reshape(rows_here, head_dim),
        value_tensor.reshape(rows_here, head_dim),
        comp_key_weight,
        comp_value_weight,
        selection[:, 0, :],
        encoded_queries,
        lax.axis_size("ctx"),
        lax.axis_size("head"),
    )
    return selected(slots, encoded_queries, kv, near, logits, block_len, picked)


def solution(mesh):
    return jax.shard_map(
        body,
        mesh=mesh,
        in_specs=(
            P("ctx", "head"),
            P("head", None),
            P("ctx", "head", None),
            P("ctx", "head", None),
            P("ctx", "head", None),
            P(),
            P(),
            P("ctx", "head", None),
        ),
        out_specs=P("ctx", "head", None),
        check_vma=False,
    )
```

```python
import functools

import jax
import jax.numpy as jnp
from jax import lax
from jax.experimental import pallas as pl
from jax.experimental.pallas import tpu as pltpu
from jax.sharding import PartitionSpec as P

WINDOW_TOKENS = 512
NEG = -1e30
LOG2E = 1.4426950408889634
F32 = jnp.float32
BF16 = jnp.bfloat16


def dot_t(a, b):
    return lax.dot_general(a, b, (((1,), (1,)), ((), ())), preferred_element_type=F32)


def split(value):
    high = value.astype(BF16)
    return jnp.concatenate([high, (value - high.astype(F32)).astype(BF16)], axis=1)


def token_gates(logits, heads, wanted):
    tokens, columns = logits.shape
    gates = jax.nn.sigmoid(logits)
    gates = jnp.broadcast_to(gates[:, None, :], (tokens, heads, columns))
    gates = gates.reshape(tokens * heads, columns)
    head = lax.broadcasted_iota(jnp.int32, gates.shape, 0) % heads
    branch = lax.broadcasted_iota(jnp.int32, gates.shape, 1) - 3 * head
    return [
        jnp.sum(jnp.where(branch == b, gates, 0.0), axis=1, keepdims=True) for b in wanted
    ]


def near_and_comp(q, gates, k_win, v_win, ck, cv, first_token, own_block, heads, block):
    rows_n, width = q.shape
    window = WINDOW_TOKENS
    factor = LOG2E * width**-0.5
    comp_n = ck.shape[0]
    row = lax.broadcasted_iota(jnp.int32, (rows_n, 128), 0) // heads + first_token
    col = lax.broadcasted_iota(jnp.int32, (rows_n, 128), 1)
    d = dot_t(q, k_win)
    low = window - own_block * block
    wcol = lax.broadcasted_iota(jnp.int32, (1, window - 128), 1) + 128
    head_part = jnp.where((col > row) & (col >= low), d[:, :128], NEG)
    mid_part = d[:, 128:window] + jnp.where(wcol >= low, 0.0, NEG)
    own_part = jnp.where(col[:, :block] <= row[:, :block], d[:, window:], NEG)
    d = jnp.concatenate([head_part, mid_part, own_part], axis=1)
    m = jnp.max(d, axis=1, keepdims=True)
    p = jnp.exp2((d - m) * factor).astype(BF16)
    acc = jnp.dot(p, v_win, preferred_element_type=F32)
    total = acc[:, :width] * (gates[1] / acc[:, width:])
    d = dot_t(jnp.concatenate([q, q], axis=1), ck)
    crow = lax.broadcasted_iota(jnp.int32, (rows_n, comp_n), 0) // heads + first_token
    ccol = lax.broadcasted_iota(jnp.int32, (rows_n, comp_n), 1)
    d = jnp.where((ccol + 1) * block - 1 <= crow + own_block * block, d, NEG)
    m = jnp.maximum(jnp.max(d, axis=1, keepdims=True), 0.0)
    p = jnp.exp2((d - m) * factor)
    sums = jnp.sum(p, axis=1, keepdims=True) + jnp.exp2(-m * factor)
    acc = jnp.dot(p.astype(BF16), cv, preferred_element_type=F32)
    return total + (acc[:, :width] + acc[:, width:]) * (gates[0] / sums)


SLOTS = 4
VMEM_BYTES = 62 * 1024 * 1024
MESH = pl.DeviceIdType.MESH


def exchange_kernel(
    hidden_ref,
    weight_ref,
    key_ref,
    value_ref,
    comp_key_ref,
    comp_value_ref,
    short_ref,
    query_ref,
    kv_ref,
    near_ref,
    logit_ref,
    slot_ref,
    hidden,
    queries,
    keys,
    values,
    sel_ref,
    sums_ref,
    ck_ref,
    cv_ref,
    lists,
    stage,
    partial,
    parts,
    list_send,
    list_recv,
    data_send,
    data_recv,
    sums_send,
    sums_recv,
    part_send,
    part_recv,
    win_send,
    win_recv,
    load_sem,
    near_buf,
    near_sem,
):
    count = lax.axis_size("ctx")
    head_count = lax.axis_size("head")
    me = lax.axis_index("ctx")
    my_head = lax.axis_index("head")
    rows, width = key_ref.shape
    block = comp_key_ref.shape[0]
    heads = query_ref.shape[1]
    blocks = rows // block
    per = SLOTS * block
    base = count * per
    columns = logit_ref.shape[1]

    loads = [
        pltpu.make_async_copy(source, target, load_sem.at[n])
        for n, (source, target) in enumerate(
            ((key_ref, keys), (value_ref, values), (hidden_ref, hidden), (query_ref, queries))
        )
    ]
    for load in loads:
        load.start()
    barrier = pltpu.get_barrier_semaphore()

    def greet(off, carry):
        pl.semaphore_signal(
            barrier, inc=1, device_id={"ctx": lax.rem(me + off, count)}, device_id_type=MESH
        )
        return carry

    lax.fori_loop(1, count, greet, 0)
    for off in range(1, head_count):
        pl.semaphore_signal(
            barrier,
            inc=1,
            device_id={"head": lax.rem(my_head + off, head_count)},
            device_id_type=MESH,
        )
    short = short_ref[...]
    sel_ref[...] = jnp.full(sel_ref.shape, -1, jnp.int32)
    sel_ref[:, : short.shape[1]] = short
    loads[0].wait()
    loads[1].wait()
    kv_ref[pl.ds(base + rows, rows), :width] = keys[...]
    kv_ref[pl.ds(base + rows, rows), width:] = values[...]
    comp_weights = jnp.concatenate([comp_key_ref[...], comp_value_ref[...]], axis=1)
    summary = jnp.concatenate(
        [
            jnp.sum(
                kv_ref[base + rows + n * block : base + rows + (n + 1) * block, :].astype(F32)
                * comp_weights,
                axis=0,
                keepdims=True,
            )
            for n in range(blocks)
        ],
        axis=0,
    )
    sums_ref[me] = summary

    @pl.when(me == 0)
    def _():
        kv_ref[base : base + rows, :] = jnp.zeros((rows, 2 * width), BF16)

    def clear(j, carry):
        sums_ref[j] = jnp.zeros(summary.shape, F32)
        return carry

    lax.fori_loop(me + 1, count, clear, 0)
    pl.semaphore_wait(barrier, count - 1 + head_count - 1)

    def list_copy(source, target):
        return pltpu.make_async_remote_copy(
            src_ref=sel_ref,
            dst_ref=lists.at[source],
            send_sem=list_send.at[target],
            recv_sem=list_recv.at[source],
            device_id={"ctx": target},
            device_id_type=MESH,
        )

    def sums_copy(source, target):
        return pltpu.make_async_remote_copy(
            src_ref=sums_ref.at[source],
            dst_ref=sums_ref.at[source],
            send_sem=sums_send.at[target],
            recv_sem=sums_recv.at[source],
            device_id={"ctx": target},
            device_id_type=MESH,
        )

    def data_copy(source, target):
        return pltpu.make_async_remote_copy(
            src_ref=stage.at[target],
            dst_ref=kv_ref.at[pl.ds(pl.multiple_of(source * per, per), per)],
            send_sem=data_send.at[target],
            recv_sem=data_recv.at[source],
            device_id={"ctx": target},
            device_id_type=MESH,
        )

    def window_copy(target):
        return pltpu.make_async_remote_copy(
            src_ref=kv_ref.at[pl.ds(base + rows, rows)],
            dst_ref=kv_ref.at[pl.ds(base, rows)],
            send_sem=win_send,
            recv_sem=win_recv,
            device_id={"ctx": target},
            device_id_type=MESH,
        )

    def part_copy(source, target):
        return pltpu.make_async_remote_copy(
            src_ref=partial.at[target],
            dst_ref=parts.at[source],
            send_sem=part_send.at[target],
            recv_sem=part_recv.at[source],
            device_id={"head": target},
            device_id_type=MESH,
        )

    def each(first, last, step):
        def run(j, carry):
            step(j)
            return carry

        lax.fori_loop(first, last, run, 0)

    each(0, me, lambda j: list_copy(me, j).start())

    @pl.when(me < count - 1)
    def _():
        window_copy(me + 1).start()

    each(me + 1, count, lambda j: sums_copy(me, j).start())

    loads[2].wait()
    logits = dot_t(weight_ref[...], hidden[...])
    for h in range(head_count):
        partial[h] = logits[h * columns : (h + 1) * columns, :]
    for off in range(1, head_count):
        part_copy(my_head, lax.rem(my_head + off, head_count)).start()

    def pack(step, carry):
        target = count - 1 - step
        list_copy(target, me).wait_recv()
        wanted = lists[target]
        rank = jnp.zeros((1, 1), F32)
        places = []
        for n in range(blocks):
            need = jnp.max(
                jnp.where(wanted == me * blocks + n, 1.0, 0.0), axis=(0, 1), keepdims=True
            )
            places.append(jnp.where(need > 0, rank, -1.0))
            rank = rank + need
        for s in range(SLOTS):
            packed = jnp.zeros((block, 2 * width), BF16)
            for n in range(blocks):
                rows_n = kv_ref[base + rows + n * block : base + rows + (n + 1) * block, :]
                chosen = jnp.where(places[n] == s, 1.0, 0.0)
                packed += rows_n * jnp.broadcast_to(chosen, rows_n.shape).astype(BF16)
            stage[target, s * block : (s + 1) * block, :] = packed
        return carry

    lax.fori_loop(0, count - 2 - me, pack, 0)

    @pl.when(me > 0)
    def _():
        window_copy(me).wait_recv()

    @pl.when(me < count - 1)
    def _():
        list_copy(me + 1, me).wait_recv()
        window_copy(me + 1).wait_send()

    def send(step, carry):
        data_copy(me, count - 1 - step).start()
        return carry

    lax.fori_loop(0, count - 2 - me, send, 0)

    mine = sel_ref[...]
    query = lax.broadcasted_iota(jnp.int32, mine.shape, 0) + me * blocks

    def place(j, slots):
        rank = jnp.zeros((1, 1), F32)
        for n in range(blocks):
            named = mine == j * blocks + n
            need = jnp.max(jnp.where(named, 1.0, 0.0), axis=(0, 1), keepdims=True)
            packed = rank.astype(jnp.int32) + j * SLOTS
            whole = count * SLOTS + n + (j - me + 1) * blocks
            place_n = jnp.where(j < me - 1, packed, whole)
            slots = jnp.where(named & (j * blocks + n <= query), place_n, slots)
            rank = rank + need
        return slots

    slot_ref[...] = lax.fori_loop(0, me + 1, place, jnp.full(mine.shape, -1, jnp.int32))

    for off in range(1, head_count):
        part_copy(lax.rem(my_head + off, head_count), my_head).wait_recv()
    total = partial[my_head]
    for off in range(1, head_count):
        total += parts[lax.rem(my_head + off, head_count)]
    logit_ref[...] = total.T

    each(0, me, lambda j: sums_copy(j, me).wait_recv())
    sums = sums_ref[...].reshape(ck_ref.shape)
    ck_ref[...] = split(sums[:, :width])
    cv_ref[...] = split(sums[:, width:])
    loads[3].wait()
    tokens = 32

    def near_copy(n):
        at = pl.ds(pl.multiple_of(n * block, block), block)
        return pltpu.make_async_copy(near_buf.at[at], near_ref.at[at], near_sem.at[n])

    def near(n, carry):
        start = base + rows + n * block - WINDOW_TOKENS
        k_win = kv_ref[pl.ds(pl.multiple_of(start, block), WINDOW_TOKENS + block), :width]
        v_win = kv_ref[pl.ds(pl.multiple_of(start, block), WINDOW_TOKENS + block), width:]
        v_win = jnp.concatenate([v_win, jnp.ones_like(v_win)], axis=1)
        for c in range(block // tokens):
            at = pl.ds(pl.multiple_of(n * block + c * tokens, tokens), tokens)
            result = near_and_comp(
                queries[at].reshape(tokens * heads, width),
                token_gates(logit_ref[at, :], heads, (0, 2)),
                k_win,
                v_win,
                ck_ref[...],
                cv_ref[...],
                c * tokens,
                me * blocks + n,
                heads,
                block,
            )
            near_buf[at] = result.reshape(tokens, heads, width)
        near_copy(n).start()
        return carry

    lax.fori_loop(0, blocks, near, 0)
    each(0, me - 1, lambda j: data_copy(j, me).wait_recv())
    each(0, me, lambda j: list_copy(me, j).wait_send())
    each(me + 1, count, lambda j: sums_copy(me, j).wait_send())
    each(me + 2, count, lambda j: data_copy(me, j).wait_send())
    each(0, blocks, lambda n: near_copy(n).wait())

    for off in range(1, head_count):
        part_copy(my_head, lax.rem(my_head + off, head_count)).wait_send()


def exchange(hidden, weight, keys, values, comp_key, comp_value, lists, queries, count, head_count):
    rows, width = keys.shape
    block = comp_key.shape[0]
    blocks = rows // block
    columns = weight.shape[0] // head_count
    padded = (blocks, 128)
    per = SLOTS * block
    whole = pl.BlockSpec(memory_space=pltpu.VMEM)
    far = pl.BlockSpec(memory_space=pltpu.HBM)
    dma = pltpu.SemaphoreType.DMA
    return pl.pallas_call(
        exchange_kernel,
        out_shape=(
            jax.ShapeDtypeStruct((count * per + 2 * rows, 2 * width), BF16),
            jax.ShapeDtypeStruct(queries.shape, F32),
            jax.ShapeDtypeStruct((rows, columns), F32),
            jax.ShapeDtypeStruct(padded, jnp.int32),
        ),
        in_specs=[far, whole, far, far, whole, whole, whole, far],
        out_specs=(whole, far, whole, whole),
        scratch_shapes=[
            pltpu.VMEM(hidden.shape, BF16),
            pltpu.VMEM(queries.shape, BF16),
            pltpu.VMEM(keys.shape, BF16),
            pltpu.VMEM(values.shape, BF16),
            pltpu.VMEM(padded, jnp.int32),
            pltpu.VMEM((count, blocks, 2 * width), F32),
            pltpu.VMEM((count * blocks, 2 * width), BF16),
            pltpu.VMEM((count * blocks, 2 * width), BF16),
            pltpu.VMEM((count,) + padded, jnp.int32),
            pltpu.VMEM((count, per, 2 * width), BF16),
            pltpu.VMEM((head_count, columns, rows), F32),
            pltpu.VMEM((head_count, columns, rows), F32),
            dma((count,)),
            dma((count,)),
            dma((count,)),
            dma((count,)),
            dma((count,)),
            dma((count,)),
            dma((head_count,)),
            dma((head_count,)),
            dma,
            dma,
            dma((4,)),
            pltpu.VMEM(queries.shape, F32),
            dma((blocks,)),
        ],
        compiler_params=pltpu.CompilerParams(
            collective_id=0, has_side_effects=True, vmem_limit_bytes=VMEM_BYTES
        ),
        cost_estimate=pl.CostEstimate(
            flops=3_000_000_000, bytes_accessed=6_000_000, transcendentals=5_000_000
        ),
    )(hidden, weight, keys, values, comp_key, comp_value, lists, queries)


def selected_kernel(slot_ref, q_ref, kv_ref, near_ref, logit_ref, out_ref, k_sel, v_sel):
    block, heads, width = q_ref.shape
    picked = k_sel.shape[0] // block
    num = pl.program_id(0)
    factor = LOG2E * width**-0.5
    shard = pl.num_programs(0) * block
    own_start = pl.multiple_of(kv_ref.shape[0] - shard + num * block, block)
    own_rows = kv_ref[pl.ds(own_start, block), :]
    k_sel[0:block, :] = own_rows[:, :width]
    v_sel[0:block, :width] = own_rows[:, width:]
    v_sel[0:block, width:] = jnp.ones((block, width), BF16)
    own_key = jnp.broadcast_to(own_rows[0:1, :width].astype(F32), (block, width)).astype(BF16)
    for k in range(1, picked):
        slot = slot_ref[num, k]
        keep = jnp.full((block, width), jnp.where(slot >= 0, 1.0, 0.0), F32).astype(BF16)
        start = pl.multiple_of(jnp.where(slot >= 0, slot * block, own_start), block)
        rows = kv_ref[pl.ds(start, block), :]
        at = slice(k * block, (k + 1) * block)
        k_sel[at, :] = rows[:, :width] * keep + own_key * (1.0 - keep)
        v_sel[at, :width] = rows[:, width:] * keep
        v_sel[at, width:] = keep
    tokens = 32
    rows_n = tokens * heads
    for c in range(block // tokens):
        at = slice(c * tokens, (c + 1) * tokens)
        q = q_ref[at].reshape(rows_n, width)
        row = lax.broadcasted_iota(jnp.int32, (rows_n, 128), 0) // heads + c * tokens
        col = lax.broadcasted_iota(jnp.int32, (rows_n, 128), 1)
        gate = token_gates(logit_ref[at, :], heads, (1,))[0]
        d = dot_t(q, k_sel[...])
        d = jnp.concatenate(
            [jnp.where((col <= row) | (col >= block), d[:, :128], NEG), d[:, 128:]], axis=1
        )
        m = jnp.max(d, axis=1, keepdims=True)
        p = jnp.exp2((d - m) * factor).astype(BF16)
        acc = jnp.dot(p, v_sel[...], preferred_element_type=F32)
        total = near_ref[at].reshape(rows_n, width) + acc[:, :width] * (gate / acc[:, width:])
        out_ref[at] = total.astype(BF16).reshape(tokens, heads, width)


def selected(slots, queries, kv, near, logits, block, picked):
    rows, heads, width = queries.shape
    blocks_here = rows // block
    whole = pl.BlockSpec(memory_space=pltpu.VMEM)
    scalars = pl.BlockSpec(memory_space=pltpu.SMEM)
    return pl.pallas_call(
        selected_kernel,
        grid=(blocks_here,),
        out_shape=jax.ShapeDtypeStruct(queries.shape, BF16),
        in_specs=[
            scalars,
            pl.BlockSpec((block, heads, width), lambda i: (i, 0, 0)),
            whole,
            pl.BlockSpec((block, heads, width), lambda i: (i, 0, 0)),
            pl.BlockSpec((block, logits.shape[1]), lambda i: (i, 0)),
        ],
        out_specs=pl.BlockSpec((block, heads, width), lambda i: (i, 0, 0)),
        scratch_shapes=[
            pltpu.VMEM((picked * block, width), BF16),
            pltpu.VMEM((picked * block, 2 * width), BF16),
        ],
        compiler_params=pltpu.CompilerParams(vmem_limit_bytes=VMEM_BYTES),
        cost_estimate=pl.CostEstimate(
            flops=4_500_000_000, bytes_accessed=8_000_000, transcendentals=9_000_000
        ),
    )(slots, queries, kv, near, logits)


def body(
    hidden_in,
    gate_weight,
    encoded_queries,
    encoded_keys,
    value_tensor,
    comp_key_weight,
    comp_value_weight,
    selection,
):
    rows_here, heads_here, head_dim = encoded_queries.shape
    block_len = comp_key_weight.shape[0]
    picked = selection.shape[-1]
    kv, near, logits, slots = exchange(
        hidden_in,
        gate_weight.T,
        encoded_keys.reshape(rows_here, head_dim),
        value_tensor.reshape(rows_here, head_dim),
        comp_key_weight,
        comp_value_weight,
        selection[:, 0, :],
        encoded_queries,
        lax.axis_size("ctx"),
        lax.axis_size("head"),
    )
    return selected(slots, encoded_queries, kv, near, logits, block_len, picked)


def solution(mesh):
    return jax.shard_map(
        body,
        mesh=mesh,
        in_specs=(
            P("ctx", "head"),
            P("head", None),
            P("ctx", "head", None),
            P("ctx", "head", None),
            P("ctx", "head", None),
            P(),
            P(),
            P("ctx", "head", None),
        ),
        out_specs=P("ctx", "head", None),
        check_vma=False,
    )
```
